256 devices in a mesh: row: 16 (over y, x), col: 8 (over z), layer: 2 (over core).
Axes of the slice: x: 4, y: 4, z: 8, core: 2. Of those that a mesh axis runs over, the one named last changes fastest.
Arguments:
- f1_vals: bfloat16 [128, 16, 128, 128], P('row', ('col', 'layer')), may hold values from -6 to 6
- f1_cols: int32 [128, 16], P('row', ('col', 'layer')), may hold values from 0 to 255, as said below
- p0_vals: bfloat16 [256, 16, 128, 128], P(('row', 'layer'), 'col'), may hold values from -0.5 to 0.5
- p0_cols: int32 [256, 16], P(('row', 'layer'), 'col'), may hold values from 0 to 255, as said below
- s_vals: bfloat16 [256, 16, 128, 128], P(('row', 'layer'), 'col'), may hold values from -0.375 to 0.375
- s_cols: int32 [256, 16], P(('row', 'layer'), 'col'), may hold values from 0 to 255, as said below
- p1_filter: int32 [128, 32], P('row', ('col', 'layer')), may hold values from 0 to 255, as said below
- q_filter: int32 [128, 16], P('row', ('col', 'layer')), may hold values from 0 to 255, as said below
Outputs:
- p1_vals: bfloat16 [128, 32, 128, 128], P('row', ('col', 'layer'))
- q_vals: bfloat16 [128, 16, 128, 128], P('row', ('col', 'layer'))
The draws below stay inside these ranges and needn't reach their ends.
Inputs may be any that keep to these rules, and one draw needn't show every extreme that they name: `f1_cols`: slot g + s of a block row names a block column J of class g, that is J % 8 == g // 2 and (J // 8) % 2 == g % 2; the 1 column of one class in one row are distinct. `p0_cols`: slot u * 2 + w of a block row names a block column J with J % 8 == u; the 2 columns of one u in one row are distinct. `s_cols`: slot u * 2 + w of a block row names a block column J with J % 8 == u; the 2 columns of one u in one row are distinct. `p1_filter`: slot g * 2 + o names a block column of class g as for f1_cols; distinct within a class and row. `q_filter`: slot g + o names a block column of class g as for f1_cols; distinct within a class and row.
All inputs are finite; a program needn't handle non-finite values.
Results may differ from the reference program's by a relative error of at most 0.0085.
Values may be sent and summed in bfloat16 or wider, within the bound.
A program may use at most 128 MiB of HBM per device.

```python
import jax
import jax.numpy as jnp
from jax import lax

BLK = 128
NBLK = 256
WA = 1
WB = 2
WS = 2
WO = 2
WQ = 1
HB = 128
TRB = 8
GROUPS = 16
MEMBERS = 16
N_COL = 8
N_LAYER = 2


def class_columns(key, row_total, per_group):
    scores = jax.random.randint(key, (row_total, GROUPS, MEMBERS), 0, 1 << 20) * MEMBERS + jnp.arange(MEMBERS, dtype=jnp.int32)
    scores = scores.at[0, :, 0].set(-1)
    scores = scores.at[row_total - 1, :, MEMBERS - 1].set(-1)
    ranking = jnp.argsort(scores, axis=-1)[:, :, :per_group].astype(jnp.int32)
    group_ids = jnp.arange(GROUPS, dtype=jnp.int32)[None, :, None]
    col_class = group_ids // N_LAYER
    layer_class = group_ids % N_LAYER
    per_tile = TRB // N_COL
    row_tile = ranking // per_tile
    within = ranking % per_tile
    columns = (row_tile * N_LAYER + layer_class) * TRB + col_class + N_COL * within
    return columns.reshape(row_total, GROUPS * per_group).astype(jnp.int32)


def grid_columns(key, row_total, per_group):
    width = NBLK // N_COL
    scores = jax.random.randint(key, (row_total, N_COL, width), 0, 1 << 20) * width + jnp.arange(width, dtype=jnp.int32)
    scores = scores.at[0, :, 0].set(-1)
    scores = scores.at[row_total - 1, :, width - 1].set(-1)
    ranking = jnp.argsort(scores, axis=-1)[:, :, :per_group].astype(jnp.int32)
    columns = jnp.arange(N_COL, dtype=jnp.int32)[None, :, None] + N_COL * ranking
    return columns.reshape(row_total, N_COL * per_group).astype(jnp.int32)


def draw_f1_cols(key, part):
    key = jax.random.fold_in(key, 11)
    return class_columns(key, HB, WA)


def draw_p0_cols(key, part):
    key = jax.random.fold_in(key, 12)
    return grid_columns(key, NBLK, WB)


def draw_s_cols(key, part):
    key = jax.random.fold_in(key, 13)
    return grid_columns(key, NBLK, WS)


def draw_p1_filter(key, part):
    key = jax.random.fold_in(key, 14)
    return class_columns(key, HB, WO)


def draw_q_filter(key, part):
    key = jax.random.fold_in(key, 15)
    return class_columns(key, HB, WQ)


def steps_of(key, dims, shards, least, largest):
    factor_of = 1.0
    for axis_at, shards_of in shards:
        steps = jax.random.uniform(jax.random.fold_in(jax.random.fold_in(key, 6), axis_at), (shards_of,), jnp.float32, least / len(shards), largest / len(shards))
        factor_of = factor_of * jnp.repeat(jnp.exp(steps), dims[axis_at] // shards_of).reshape((-1,) + (1,) * (len(dims) - 1 - axis_at))
    return factor_of


def centred(stream_key, dims, deviation, bound, cuts=(), kind=jnp.bfloat16):
    result = jax.random.normal(stream_key, dims, jnp.float32) * deviation
    if len(cuts) > 0:
        result = steps_of(stream_key, dims, cuts, -0.22, 0.18) * result
    return jnp.clip(result, min=-bound, max=bound).astype(kind)


def setup_inputs(seed: int = 0) -> dict:
    seeds = jax.random.split(jax.random.key(seed), 9)
    return {
        "f1_vals": centred(seeds[0], (HB, GROUPS * WA, BLK, BLK), 1.0, 6.0, ((0, 16), (1, 16))),
        "f1_cols": draw_f1_cols(jax.random.fold_in(seeds[8], 71), 0),
        "p0_vals": centred(seeds[2], (NBLK, N_COL * WB, BLK, BLK), BLK ** -0.5, 0.5, ((0, 32), (1, 8))),
        "p0_cols": draw_p0_cols(jax.random.fold_in(seeds[8], 71), 0),
        "s_vals": centred(seeds[4], (NBLK, N_COL * WS, BLK, BLK), (2 * BLK) ** -0.5, 0.375, ((0, 32), (1, 8))),
        "s_cols": draw_s_cols(jax.random.fold_in(seeds[8], 71), 0),
        "p1_filter": draw_p1_filter(jax.random.fold_in(seeds[8], 71), 0),
        "q_filter": draw_q_filter(jax.random.fold_in(seeds[8], 71), 0),
    }


def product(a_values, a_columns, b_values, b_columns, wanted_columns):
    def one_row(row_data):
        values, columns, wanted = row_data
        b_rows = jnp.take(b_values, columns, axis=0).astype(jnp.float32)
        b_names = jnp.take(b_columns, columns, axis=0)
        products = jnp.einsum('sab,swbc->swac', values.astype(jnp.float32), b_rows, precision=lax.Precision.HIGHEST)
        pairing = (b_names[:, :, None] == wanted[None, None, :]).astype(jnp.float32)
        return jnp.einsum('swo,swac->oac', pairing, products, precision=lax.Precision.HIGHEST)
    return lax.map(one_row, (a_values, a_columns, wanted_columns)).astype(jnp.bfloat16)


def reference(f1_vals, f1_cols, p0_vals, p0_cols, s_vals, s_cols, p1_filter, q_filter):
    p1_vals = product(f1_vals, f1_cols, p0_vals, p0_cols, p1_filter)
    q_vals = product(p1_vals, p1_filter, s_vals, s_cols, q_filter)
    return p1_vals, q_vals
```

```python
import jax
import jax.numpy as jnp
from jax import lax
from jax.experimental import pallas as pl
from jax.experimental.pallas import tpu as pltpu
from jax.sharding import PartitionSpec as P

MESH = pl.DeviceIdType.MESH
B = 128
SIDE = 4
NZ = 8
ROWS = 8
TILES = SIDE * SIDE
ZERO = TILES * 16
F1C, P0C, SC, P1F, QF = 0, 1, 3, 5, 7


def body_kernel(
    meta_ref, f1_ref, p0_ref, s_ref, p1_ref, q_ref,
    pan, span, f1_all, p1_all, rhs, rhs_q, part, part_in, q_part, q_in,
    meta_row, meta_z, meta_core, row_s, z_s, core_s,
    local_sem, meta_send, meta_recv, pan_send, pan_recv, f1_send, f1_recv,
    part_send, part_recv, p1_send, p1_recv, q_send, q_recv, smem_sem,
):
    r = lax.axis_index("row")
    u = lax.axis_index("col")
    layer = lax.axis_index("layer")
    x, y = r % SIDE, r // SIDE
    other = 1 - layer

    def chip(y_at, x_at):
        return (y_at % SIDE) * SIDE + x_at % SIDE

    own = [
        pltpu.make_async_copy(p0_ref, pan.at[pl.ds(r * 16, 16)], local_sem.at[0]),
        pltpu.make_async_copy(f1_ref, f1_all.at[pl.ds(u * 8, 8)], local_sem.at[1]),
        pltpu.make_async_copy(s_ref, span.at[pl.ds(r * 16, 16)], local_sem.at[2]),
    ]
    for copy in own:
        copy.start()

    barrier = pltpu.get_barrier_semaphore()
    for step in range(1, TILES):
        pl.semaphore_signal(barrier, inc=1, device_id=((r + step) % TILES, u, layer), device_id_type=MESH)
    for step in range(1, NZ):
        pl.semaphore_signal(barrier, inc=1, device_id=(r, (u + step) % NZ, layer), device_id_type=MESH)
    pl.semaphore_signal(barrier, inc=1, device_id=(r, u, other), device_id_type=MESH)

    pan[ZERO] = jnp.zeros((B, B), jnp.bfloat16)
    span[ZERO] = jnp.zeros((B, B), jnp.bfloat16)
    meta_row[r] = meta_ref[...]
    meta_z[u] = meta_ref[...]
    meta_core[layer] = meta_ref[...]
    pl.semaphore_wait(barrier, TILES - 1 + NZ - 1 + 1)

    sent = []

    def send(src, dst, send_sem, recv_sem, device):
        copy = pltpu.make_async_remote_copy(
            src_ref=src, dst_ref=dst, send_sem=send_sem, recv_sem=recv_sem,
            device_id=device, device_id_type=MESH,
        )
        copy.start()
        sent.append(copy)

    def arrived(dst, send_sem, recv_sem, device):
        pltpu.make_async_remote_copy(
            src_ref=dst, dst_ref=dst, send_sem=send_sem, recv_sem=recv_sem,
            device_id=device, device_id_type=MESH,
        ).wait_recv()

    for step in range(1, TILES):
        send(meta_ref, meta_row.at[r], meta_send.at[step], meta_recv.at[step], ((r + step) % TILES, u, layer))
    for step in range(1, NZ):
        at = TILES + step
        send(meta_ref, meta_z.at[u], meta_send.at[at], meta_recv.at[at], (r, (u + step) % NZ, layer))
    send(meta_ref, meta_core.at[layer], meta_send.at[0], meta_recv.at[0], (r, u, other))

    ways = ((0, 1), (0, -1), (1, 1), (1, -1))

    def tile_of(q, along, across):
        first, d = ways[q]
        if first == 0:
            return chip(y - d * across, x - d * along)
        return chip(y - d * along, x - d * across)

    def target(q, phase):
        first, d = ways[q]
        if (first + phase) % 2 == 0:
            return (chip(y, x + d), u, layer)
        return (chip(y + d, x), u, layer)

    def piece(panel, q, along, across):
        return panel.at[pl.ds(tile_of(q, along, across) * 16 + q * 4, 4)]

    def panel_send(which, q, phase, step, j):
        panel = (pan, span)[which]
        at = step if phase == 0 else 3 + step * 4 + j
        part_of = piece(panel, q, step, 0) if phase == 0 else piece(panel, q, j, step)
        send(part_of, part_of, pan_send.at[which, q, at], pan_recv.at[which, q, at], target(q, phase))

    def panel_arrived(which, q, phase, step, j):
        panel = (pan, span)[which]
        at = step if phase == 0 else 3 + step * 4 + j
        part_of = piece(panel, q, step + 1, 0) if phase == 0 else piece(panel, q, j, step + 1)
        arrived(part_of, pan_send.at[which, q, at], pan_recv.at[which, q, at], target(q, phase))

    def panel_begin(which):
        for q in range(4):
            panel_send(which, q, 0, 0, 0)
        for q in range(4):
            panel_send(which, q, 1, 0, 0)

    def panel_round(which, n):
        for q in range(4):
            if n < 3:
                panel_arrived(which, q, 0, n, 0)
                if n < 2:
                    panel_send(which, q, 0, n + 1, 0)
                panel_send(which, q, 1, 0, n + 1)
            else:
                step, j = (n - 3) // 4, (n - 3) % 4
                panel_arrived(which, q, 1, step, j)
                if step < 2:
                    panel_send(which, q, 1, step + 1, j)

    def z_piece(array, width, pieces, e, step):
        d = 1 - 2 * (e % 2)
        size = width // pieces
        return array.at[pl.ds(((u - d * step) % NZ) * width + e * size, size)]

    def z_send(array, width, pieces, sems, e, step):
        d = 1 - 2 * (e % 2)
        part_of = z_piece(array, width, pieces, e, step)
        send(part_of, part_of, sems[0].at[e, step], sems[1].at[e, step], (r, (u + d) % NZ, layer))

    def z_round(array, width, pieces, sems, n):
        for e in range(pieces):
            d = 1 - 2 * (e % 2)
            part_of = z_piece(array, width, pieces, e, n + 1)
            arrived(part_of, sems[0].at[e, n], sems[1].at[e, n], (r, (u + d) % NZ, layer))
            if n + 1 < NZ - 1:
                z_send(array, width, pieces, sems, e, n + 1)

    own[0].wait()
    for q in range(4):
        panel_send(0, q, 0, 0, 0)
    own[1].wait()
    f1_sems, p1_sems = (f1_send, f1_recv), (p1_send, p1_recv)
    for e in range(2):
        z_send(f1_all, 8, 2, f1_sems, e, 0)
    for q in range(4):
        panel_send(0, q, 1, 0, 0)
    own[2].wait()

    for step in range(1, TILES):
        arrived(meta_row.at[(r - step) % TILES], meta_send.at[step], meta_recv.at[step], ((r + step) % TILES, u, layer))
    for step in range(1, NZ):
        at = TILES + step
        arrived(meta_z.at[(u - step) % NZ], meta_send.at[at], meta_recv.at[at], (r, (u + step) % NZ, layer))
    arrived(meta_core.at[other], meta_send.at[0], meta_recv.at[0], (r, u, other))
    tables = [
        pltpu.make_async_copy(meta_row, row_s, smem_sem.at[0]),
        pltpu.make_async_copy(meta_z, z_s, smem_sem.at[1]),
        pltpu.make_async_copy(meta_core, core_s, smem_sem.at[2]),
    ]
    for copy in tables:
        copy.start()

    for n in range(15):
        if n == 11:
            panel_begin(1)
        panel_round(0, n)
        if n < NZ - 1:
            z_round(f1_all, 8, 2, f1_sems, n)
    for copy in tables:
        copy.wait()

    def choose(panel, index):
        return panel[index]

    def first_row(i, carry):
        for c in range(NZ):
            k = z_s[c, i, F1C]
            t = lax.shift_right_logical(k, 4)
            base = t * 16 + c * 2
            n0, n1 = row_s[t, c, P0C], row_s[t, c, P0C + 1]
            for o in range(4):
                want = core_s[o // 2, i, P1F + o % 2]
                index = jnp.where(n0 == want, base, jnp.where(n1 == want, base + 1, ZERO))
                rhs[c * B:(c + 1) * B, o * B:(o + 1) * B] = choose(pan, index)
        lhs = jnp.concatenate([f1_all[c * 8 + i] for c in range(NZ)], axis=1)
        total = jnp.dot(lhs, rhs[...], preferred_element_type=jnp.float32)
        part[0, i] = total[:, :2 * B]
        part[1, i] = total[:, 2 * B:]
        return carry

    def part_send_row(i):
        send(part.at[other, i], part_in.at[i], part_send.at[i], part_recv.at[i], (r, u, other))

    for h in range(4):
        lax.fori_loop(2 * h, 2 * h + 2, first_row, 0)
        part_send_row(2 * h)
        part_send_row(2 * h + 1)
        if h < 3:
            panel_round(1, h)

    def finish_row(i, carry):
        total = (part[layer, i] + part_in[i]).astype(jnp.bfloat16)
        for o in range(2):
            block = total[:, o * B:(o + 1) * B]
            p1_all[u * 16 + i * 2 + o] = block
            p1_ref[i, o] = block
        return carry

    for e in range(4):
        for i in (2 * e, 2 * e + 1):
            arrived(part_in.at[i], part_send.at[i], part_recv.at[i], (r, u, other))
        lax.fori_loop(2 * e, 2 * e + 2, finish_row, 0)
        z_send(p1_all, 16, 4, p1_sems, e, 0)

    for n in range(12):
        panel_round(1, n + 3)
        if n < NZ - 1:
            z_round(p1_all, 16, 4, p1_sems, n)

    def second_row(i, carry):
        for c in range(NZ):
            for a in range(2):
                k = z_s[c, i, P1F + a]
                t = lax.shift_right_logical(k, 4)
                base = t * 16 + c * 2
                n0, n1 = row_s[t, c, SC], row_s[t, c, SC + 1]
                at = c * 2 + a
                for o in range(2):
                    want = core_s[o, i, QF]
                    index = jnp.where(n0 == want, base, jnp.where(n1 == want, base + 1, ZERO))
                    rhs_q[at * B:(at + 1) * B, o * B:(o + 1) * B] = choose(span, index)
        lhs = jnp.concatenate([p1_all[c * 16 + i * 2 + a] for c in range(NZ) for a in range(2)], axis=1)
        total = jnp.dot(lhs, rhs_q[...], preferred_element_type=jnp.float32)
        q_part[0, i] = total[:, :B].astype(jnp.bfloat16)
        q_part[1, i] = total[:, B:].astype(jnp.bfloat16)
        return carry

    for h in range(2):
        lax.fori_loop(4 * h, 4 * h + 4, second_row, 0)
        rows = pl.ds(4 * h, 4)
        send(q_part.at[other, rows], q_in.at[rows], q_send.at[h], q_recv.at[h], (r, u, other))
    for h in range(2):
        rows = pl.ds(4 * h, 4)
        arrived(q_in.at[rows], q_send.at[h], q_recv.at[h], (r, u, other))
        both = q_part[layer, rows].astype(jnp.float32) + q_in[rows].astype(jnp.float32)
        q_ref[rows] = both.astype(jnp.bfloat16)
    for copy in sent:
        copy.wait_send()


def body(f1_vals, f1_cols, p0_vals, p0_cols, s_vals, s_cols, p1_filter, q_filter):
    meta = jnp.concatenate([f1_cols, p0_cols, s_cols, p1_filter, q_filter], axis=1)
    meta = jnp.pad(meta, ((0, 0), (0, B - meta.shape[1])))
    bf16, f32, i32 = jnp.bfloat16, jnp.float32, jnp.int32
    dma = pltpu.SemaphoreType.DMA
    p1, q = pl.pallas_call(
        body_kernel,
        out_shape=(
            jax.ShapeDtypeStruct((ROWS, 2, B, B), bf16),
            jax.ShapeDtypeStruct((ROWS, B, B), bf16),
        ),
        in_specs=[pl.BlockSpec(memory_space=pltpu.VMEM)] + [pl.BlockSpec(memory_space=pl.ANY)] * 3,
        out_specs=(pl.BlockSpec(memory_space=pltpu.VMEM),) * 2,
        scratch_shapes=[
            pltpu.VMEM((TILES * 16 + 1, B, B), bf16),
            pltpu.VMEM((TILES * 16 + 1, B, B), bf16),
            pltpu.VMEM((NZ * 8, B, B), bf16),
            pltpu.VMEM((NZ * 16, B, B), bf16),
            pltpu.VMEM((NZ * B, 4 * B), bf16),
            pltpu.VMEM((NZ * 2 * B, 2 * B), bf16),
            pltpu.VMEM((2, ROWS, B, 2 * B), f32),
            pltpu.VMEM((ROWS, B, 2 * B), f32),
            pltpu.VMEM((2, ROWS, B, B), bf16),
            pltpu.VMEM((ROWS, B, B), bf16),
            pltpu.VMEM((TILES, 8, B), i32),
            pltpu.VMEM((NZ, 8, B), i32),
            pltpu.VMEM((2, 8, B), i32),
            pltpu.SMEM((TILES, 8, B), i32),
            pltpu.SMEM((NZ, 8, B), i32),
            pltpu.SMEM((2, 8, B), i32),
            dma((3,)),
            dma((TILES + NZ,)), dma((TILES + NZ,)),
            dma((2, 4, 15)), dma((2, 4, 15)),
            dma((2, NZ - 1)), dma((2, NZ - 1)),
            dma((ROWS,)), dma((ROWS,)),
            dma((4, NZ - 1)), dma((4, NZ - 1)),
            dma((2,)), dma((2,)),
            dma((3,)),
        ],
        compiler_params=pltpu.CompilerParams(
            collective_id=0, has_side_effects=True, vmem_limit_bytes=56 * 1024 * 1024
        ),
    )(
        meta,
        f1_vals.reshape(ROWS, B, B),
        p0_vals.reshape(16, B, B),
        s_vals.reshape(16, B, B),
    )
    return p1, q.reshape(ROWS, 1, B, B)


def solution(mesh):
    return jax.shard_map(
        body,
        mesh=mesh,
        in_specs=(
            P("row", ("col", "layer"), None, None),
            P("row", ("col", "layer")),
            P(("row", "layer"), "col", None, None),
            P(("row", "layer"), "col"),
            P(("row", "layer"), "col", None, None),
            P(("row", "layer"), "col"),
            P("row", ("col", "layer")),
            P("row", ("col", "layer")),
        ),
        out_specs=(P("row", ("col", "layer"), None, None), P("row", ("col", "layer"), None, None)),
        check_vma=False,
    )
```

```python
import jax
import jax.numpy as jnp
from jax import lax
from jax.experimental import pallas as pl
from jax.experimental.pallas import tpu as pltpu
from jax.sharding import PartitionSpec as P

MESH = pl.DeviceIdType.MESH
B = 128
SIDE = 4
NZ = 8
ROWS = 8
TILES = SIDE * SIDE
CAP = 12
HALF = CAP // 2
PACKED = 65
BLOCKS = PACKED + 6 * CAP
F32, I32, BF16 = jnp.float32, jnp.int32, jnp.bfloat16


def inside(index, count):
    return lax.max(lax.min(index, count - 1), 0)


def fast_kernel(
    f1c_ref, p0c_ref, sc_ref, p1f_ref, qf_ref, f1_ref, p0_ref, s_ref, p1_ref, q_ref, flag_ref,
    whole_p, whole_s, buf_p, buf_s, outs, relays, f1_all, p1_all, rhs, rhs_q, part, part_in, q_part, q_in,
    own_tile, row_tiles, z_tiles, core_tiles, demand, code, code_in, index_v, list_v, index_s, list_s,
    flag_own, flag_row, flag_z, flag_core,
    local_sem, meta_send, meta_recv, code_send, code_recv, pan_send, pan_recv, pack_send, pack_recv,
    rel_send, rel_recv, f1_send, f1_recv, part_send, part_recv, p1_send, p1_recv, q_send, q_recv,
    flag_send, flag_recv, smem_sem,
):
    r = lax.axis_index("row")
    u = lax.axis_index("col")
    layer = lax.axis_index("layer")
    x, y = r % SIDE, r // SIDE
    other = 1 - layer
    whole, bufs = (whole_p, whole_s), (buf_p, buf_s)

    def chip(y_at, x_at):
        return ((y_at % SIDE) * SIDE + x_at % SIDE, u, layer)

    own = []
    for which, ref in ((0, p0_ref), (1, s_ref)):
        own.append(pltpu.make_async_copy(ref.at[pl.ds(0, 8)], whole[which].at[pl.ds(1 + x * 8, 8)], local_sem.at[2 * which]))
        own.append(pltpu.make_async_copy(ref.at[pl.ds(8, 8)], whole[which].at[pl.ds(33 + y * 8, 8)], local_sem.at[2 * which + 1]))
    own.append(pltpu.make_async_copy(f1_ref, f1_all.at[pl.ds(u * 8, 8)], local_sem.at[4]))
    for copy in own:
        copy.start()

    barrier = pltpu.get_barrier_semaphore()
    for step in range(1, TILES):
        pl.semaphore_signal(barrier, inc=1, device_id=((r + step) % TILES, u, layer), device_id_type=MESH)
    for step in range(1, NZ):
        pl.semaphore_signal(barrier, inc=1, device_id=(r, (u + step) % NZ, layer), device_id_type=MESH)
    pl.semaphore_signal(barrier, inc=1, device_id=(r, u, other), device_id_type=MESH)

    for panel in whole:
        panel[0] = jnp.zeros((B, B), BF16)
    sub8 = lax.broadcasted_iota(I32, (8, B), 0)
    lane8 = lax.broadcasted_iota(I32, (8, B), 1)

    own_tile[...] = jnp.full((8, B), -1, I32)
    for at, ref in ((0, p0c_ref), (2, sc_ref), (4, f1c_ref), (5, p1f_ref), (7, qf_ref)):
        own_tile[at:at + ref.shape[0], 0:8] = ref[...]
    row_tiles[r] = own_tile[...]
    z_tiles[u] = own_tile[...]
    core_tiles[layer] = own_tile[...]
    pl.semaphore_wait(barrier, TILES - 1 + NZ - 1 + 1)

    sent = []

    def remote(src, dst, send_sem, recv_sem, device):
        return pltpu.make_async_remote_copy(
            src_ref=src, dst_ref=dst, send_sem=send_sem, recv_sem=recv_sem,
            device_id=device, device_id_type=MESH,
        )

    def send(src, dst, send_sem, recv_sem, device):
        copy = remote(src, dst, send_sem, recv_sem, device)
        copy.start()
        sent.append(copy)

    def arrived(dst, send_sem, recv_sem, device):
        remote(dst, dst, send_sem, recv_sem, device).wait_recv()

    def row_peer(step):
        return ((r + step) % TILES, u, layer)

    def z_peer(step):
        return (r, (u + step) % NZ, layer)

    core_peer = (r, u, other)

    for step in range(1, NZ):
        at = TILES + step
        send(own_tile, z_tiles.at[u], meta_send.at[at], meta_recv.at[at], z_peer(step))
    send(own_tile, core_tiles.at[layer], meta_send.at[0], meta_recv.at[0], core_peer)
    for step in range(1, TILES):
        send(own_tile, row_tiles.at[r], meta_send.at[step], meta_recv.at[step], row_peer(step))

    def along(axis, d):
        return chip(y, x + d) if axis == 0 else chip(y + d, x)

    def quarter(which, h, q, d):
        at = (x if h == 0 else y) - d
        return whole[which].at[pl.ds(1 + 32 * h + (at % SIDE) * 8 + q * 4, 4)]

    def panel_begin(which):
        for n in range(2):
            for h in range(2):
                for way in (0, 1):
                    q, d = n if way == 0 else 1 - n, 1 - 2 * way
                    part_of = quarter(which, h, q, 0)
                    send(part_of, part_of, pan_send.at[which, h, way, n], pan_recv.at[which, h, way, n], along(h, d))

    def panel_round(which, n):
        for h in range(2):
            for way in (0, 1):
                d = 1 - 2 * way
                q = (n if way == 0 else 1 - n) if n < 2 else way
                part_of = quarter(which, h, q, d if n < 2 else 2 * d)
                arrived(part_of, pan_send.at[which, h, way, n], pan_recv.at[which, h, way, n], along(h, d))
                if n == 0:
                    send(part_of, part_of, pan_send.at[which, h, way, 2], pan_recv.at[which, h, way, 2], along(h, d))

    def packet(which, h, d):
        return bufs[which].at[pl.ds(PACKED + (h * 3 + d - 1) * CAP, CAP)]

    def half_of(ref, e):
        return ref.at[pl.ds(e * HALF, HALF)]

    def relay(which):
        for h in range(2):
            for e, way in ((0, 1), (1, -1)):
                arrived(relays.at[which, h, e], rel_send.at[which, h, e], rel_recv.at[which, h, e], along(1 - h, way))
                send(
                    relays.at[which, h, e], half_of(packet(which, h, 2), e),
                    pack_send.at[which, h, 3 + e], pack_recv.at[which, h, 3 + e], along(1 - h, way),
                )

    def packets_arrived(which):
        for h in range(2):
            for d in (1, 3):
                arrived(packet(which, h, d), pack_send.at[which, h, d - 1], pack_recv.at[which, h, d - 1], along(1 - h, 1))
            for e in range(2):
                arrived(half_of(packet(which, h, 2), e), pack_send.at[which, h, 3 + e], pack_recv.at[which, h, 3 + e], along(1 - h, 1))

    def z_piece(array, width, pieces, e, step):
        d = 1 - 2 * (e % 2)
        size = width // pieces
        return array.at[pl.ds(((u - d * step) % NZ) * width + e * size, size)]

    def z_send(array, width, pieces, sems, e, step):
        d = 1 - 2 * (e % 2)
        part_of = z_piece(array, width, pieces, e, step)
        send(part_of, part_of, sems[0].at[e, step], sems[1].at[e, step], z_peer(d))

    def z_round(array, width, pieces, sems, n, only=None):
        for e in range(pieces) if only is None else only:
            d = 1 - 2 * (e % 2)
            arrived(z_piece(array, width, pieces, e, n + 1), sems[0].at[e, n], sems[1].at[e, n], z_peer(d))
            if n + 1 < NZ - 1:
                z_send(array, width, pieces, sems, e, n + 1)

    f1_sems, p1_sems = (f1_send, f1_recv), (p1_send, p1_recv)
    own[0].wait()
    own[1].wait()
    panel_begin(0)
    own[4].wait()
    for e in range(4):
        z_send(f1_all, 8, 4, f1_sems, e, 0)
    own[2].wait()
    own[3].wait()

    for step in range(1, NZ):
        at = TILES + step
        arrived(z_tiles.at[(u - step) % NZ], meta_send.at[at], meta_recv.at[at], z_peer(step))
    arrived(core_tiles.at[other], meta_send.at[0], meta_recv.at[0], core_peer)

    def column_of(line):
        spread = jnp.where(sub8 == lane8, jnp.broadcast_to(line.astype(F32), (8, B)), 0.0)
        return jnp.broadcast_to(jnp.sum(spread, axis=1, keepdims=True), (8, B))

    for at in range(3):
        merged = jnp.zeros((8, B), F32)
        for c in range(NZ):
            merged = jnp.where(lane8 == c, column_of(z_tiles[c, 4 + at:5 + at, :]), merged)
        demand[at] = merged.astype(I32)
    for o in range(4):
        demand[3 + o] = column_of(core_tiles[o // 2, 5 + o % 2:6 + o % 2, :]).astype(I32)
    for o in range(2):
        demand[7 + o] = column_of(core_tiles[o, 7:8, :]).astype(I32)

    for step in range(1, TILES):
        arrived(row_tiles.at[(r - step) % TILES], meta_send.at[step], meta_recv.at[step], row_peer(step))

    tile = lax.broadcasted_iota(I32, (TILES, B), 0)
    lane = lax.broadcasted_iota(I32, (TILES, B), 1)
    tile_y, tile_x = lax.shift_right_logical(tile, 2), tile & 3
    upper = lane >= 4
    lane_a = lax.broadcasted_iota(I32, (B, B), 0)
    lane_b = lax.broadcasted_iota(I32, (B, B), 1)
    same = lax.shift_right_logical(lane_a, 2) == lax.shift_right_logical(lane_b, 2)
    one, nil = jnp.ones((), F32), jnp.zeros((), F32)
    lanes_all = jnp.where(same, one, nil)
    lanes_before = jnp.where(same & (lane_a < lane_b), one, nil)
    tile_a = lax.broadcasted_iota(I32, (TILES, TILES), 0)
    tile_b = lax.broadcasted_iota(I32, (TILES, TILES), 1)
    before = tile_b < tile_a
    same_y = lax.shift_right_logical(tile_a, 2) == lax.shift_right_logical(tile_b, 2)
    same_x = (tile_a & 3) == (tile_b & 3)
    tiles_y = jnp.where(before & same_y, one, nil)
    tiles_x = jnp.where(before & same_x, one, nil)

    def dot(a, b):
        return jnp.dot(a, b, preferred_element_type=F32)

    name = [[row_tiles[:, 2 * which + w, :] for w in range(2)] for which in range(2)]

    def wide(at, i):
        return jnp.broadcast_to(demand[at, i:i + 1, :], (TILES, B))

    def matches(which):
        result = []
        for i in range(ROWS):
            wants = [wide(at, i) for at in (range(3, 7) if which == 0 else range(7, 9))]
            for at in (range(1) if which == 0 else range(1, 3)):
                hit = lax.shift_right_logical(wide(at, i), 4) == tile
                result.append([[hit & (name[which][w] == want) for w in range(2)] for want in wants])
        return result

    def needs(masks):
        total = []
        for w in range(2):
            need = masks[0][0][w]
            for row in masks:
                for slot in row:
                    need = need | slot[w]
            total.append(jnp.where(need, one, nil))
        return total

    def ranks(need):
        both = need[0] + need[1]
        all_of = dot(both, lanes_all)
        first = jnp.where(upper, dot(tiles_x, all_of), dot(tiles_y, all_of)) + dot(both, lanes_before)
        return [first, first + need[0]]

    within = (lane & 3) * 2
    place = 1 + jnp.where(upper, 32 + tile_y * 8 + within, tile_x * 8 + within)
    offset = jnp.where(upper, tile_x - x, tile_y - y) & 3
    here = offset == 0
    packed = PACKED + jnp.where(upper, 3 * CAP, 0) + (offset - 1) * CAP
    place_f, packed_f = place.astype(F32), packed.astype(F32)

    def own_code(which):
        masks = matches(which)
        need = needs(masks)
        rank = ranks(need)
        code[which] = (jnp.where(need[0] > 0.5, rank[0] + 1.0, 0.0) + 64.0 * jnp.where(need[1] > 0.5, rank[1] + 1.0, 0.0)).astype(I32)
        for axis in range(2):
            for d in (1, 2, 3):
                at = axis * 3 + d - 1
                send(
                    code.at[which], code_in.at[which, axis, 3 - d],
                    code_send.at[which, at], code_recv.at[which, axis * 3 + 3 - d], along(axis, d),
                )
        return masks, need, rank

    def own_index(which, masks, need, rank):
        spot, worst = [], jnp.zeros((TILES, B), F32)
        for w in range(2):
            fits = rank[w] < float(CAP)
            spot.append(jnp.where(here, place_f + float(w), jnp.where(fits, packed_f + rank[w], 0.0)))
            worst = worst + jnp.where((need[w] > 0.5) & jnp.logical_not(fits | here), one, nil)
        at = 0
        for row in masks:
            for slot in row:
                chosen = jnp.where(slot[0], spot[0], jnp.where(slot[1], spot[1], 0.0))
                line = jnp.sum(chosen, axis=0, keepdims=True)
                index_v[which, at:at + 1, :] = line.astype(I32)
                at += 1
        return worst

    def peer_lists(which):
        table = jnp.zeros((TILES, B), F32)
        for h in range(2):
            axis = 1 - h
            mine = (jnp.logical_not(upper) & (tile_y == y)) if h == 0 else (upper & (lane < 8) & (tile_x == x))
            for d in (1, 2, 3):
                at = axis * 3 + d - 1
                arrived(code_in.at[which, axis, d - 1], code_send.at[which, at], code_recv.at[which, at], along(axis, d))
                there = jnp.where(mine, code_in[which, axis, d - 1], 0)
                rank = [there & 63, lax.shift_right_logical(there, 6)]
                slots = jnp.zeros((TILES, B), F32)
                for j in range(CAP):
                    chosen = jnp.where(rank[0] == j + 1, place_f, 0.0) + jnp.where(rank[1] == j + 1, place_f + 1.0, 0.0)
                    line = jnp.sum(chosen, axis=0, keepdims=True)
                    slots = jnp.where(tile == j, jnp.broadcast_to(line, (TILES, B)), slots)
                column = jnp.broadcast_to(jnp.sum(slots, axis=1, keepdims=True), (TILES, B))
                table = jnp.where(lane == (which * 2 + h) * 3 + d - 1, column, table)
        return table

    found = own_code(0)
    found_s = own_code(1)
    panel_round(0, 0)
    z_round(f1_all, 8, 4, f1_sems, 0)
    lists = [pltpu.make_async_copy(list_v.at[w], list_s.at[w], smem_sem.at[w]) for w in range(2)]
    list_v[0] = peer_lists(0).astype(I32)
    lists[0].start()
    z_round(f1_all, 8, 4, f1_sems, 1)
    panel_round(0, 1)
    panel_round(0, 2)
    settle = [pltpu.make_async_copy(whole[w], bufs[w].at[pl.ds(0, PACKED)], local_sem.at[5 + w]) for w in range(2)]
    z_round(f1_all, 8, 4, f1_sems, 2)
    lists[0].wait()

    def pack(which, ref):
        for h in range(2):
            for d in (2, 1, 3):
                column = (which * 2 + h) * 3 + d - 1
                for j in range(CAP):
                    outs[which, h, d - 1, j] = whole[which][inside(ref[j, column], PACKED)]
                axis = 1 - h
                if d == 2:
                    for e, way in ((0, 1), (1, -1)):
                        send(
                            half_of(outs.at[which, h, 1], e), relays.at[which, h, e],
                            rel_send.at[which, h, e], rel_recv.at[which, h, e], along(axis, way),
                        )
                else:
                    way = 1 if d == 1 else -1
                    send(
                        outs.at[which, h, d - 1], packet(which, h, 4 - d),
                        pack_send.at[which, h, d - 1], pack_recv.at[which, h, 3 - d], along(axis, way),
                    )

    pack(0, list_s.at[0])
    settle[0].start()
    z_round(f1_all, 8, 4, f1_sems, 3)
    over = own_index(0, *found)
    first_index = pltpu.make_async_copy(index_v.at[0], index_s.at[0], smem_sem.at[2])
    first_index.start()
    list_v[1] = peer_lists(1).astype(I32)
    lists[1].start()
    z_round(f1_all, 8, 4, f1_sems, 4)
    relay(0)
    panel_begin(1)
    z_round(f1_all, 8, 4, f1_sems, 5)
    over = over + own_index(1, *found_s)
    second_index = pltpu.make_async_copy(index_v.at[1], index_s.at[1], smem_sem.at[3])
    second_index.start()
    flag_own[0] = over[:8] + over[8:]
    z_round(f1_all, 8, 4, f1_sems, 6)
    first_index.wait()
    settle[0].wait()
    packets_arrived(0)
    lists[1].wait()

    def first_row(i, carry):
        for c in range(NZ):
            for o in range(4):
                rhs[c * B:(c + 1) * B, o * B:(o + 1) * B] = buf_p[inside(index_s[0, i * 4 + o, c], BLOCKS)]
        lhs = jnp.concatenate([f1_all[c * 8 + i] for c in range(NZ)], axis=1)
        total = dot(lhs, rhs[...])
        part[0, i] = total[:, :2 * B]
        part[1, i] = total[:, 2 * B:]
        return carry

    def part_send_row(i):
        send(part.at[other, i], part_in.at[i], part_send.at[i], part_recv.at[i], core_peer)

    def finish_row(i, carry):
        total = (part[layer, i] + part_in[i]).astype(BF16)
        for o in range(2):
            block = total[:, o * B:(o + 1) * B]
            p1_all[u * 16 + i * 2 + o] = block
            p1_ref[i, o] = block
        return carry

    def finish(e):
        for i in (2 * e, 2 * e + 1):
            arrived(part_in.at[i], part_send.at[i], part_recv.at[i], core_peer)
        lax.fori_loop(2 * e, 2 * e + 2, finish_row, 0)
        z_send(p1_all, 16, 4, p1_sems, e, 0)

    for h in range(4):
        lax.fori_loop(2 * h, 2 * h + 2, first_row, 0)
        part_send_row(2 * h)
        part_send_row(2 * h + 1)
        if h > 0:
            finish(h - 1)
    finish(3)

    for step in range(1, TILES):
        send(flag_own.at[0], flag_row.at[step - 1], flag_send.at[step - 1], flag_recv.at[step - 1], row_peer(step))
    z_round(p1_all, 16, 4, p1_sems, 0)
    for n in range(3):
        panel_round(1, n)
    pack(1, list_s.at[1])
    settle[1].start()
    z_round(p1_all, 16, 4, p1_sems, 1)
    total = flag_own[0]
    for step in range(1, TILES):
        arrived(flag_row.at[step - 1], flag_send.at[step - 1], flag_recv.at[step - 1], row_peer(step))
        total = total + flag_row[step - 1]
    flag_own[1] = total
    for step in range(1, NZ):
        at = TILES - 2 + step
        send(flag_own.at[1], flag_z.at[step - 1], flag_send.at[at], flag_recv.at[at], z_peer(step))
    z_round(p1_all, 16, 4, p1_sems, 2)
    relay(1)
    z_round(p1_all, 16, 4, p1_sems, 3)
    for step in range(1, NZ):
        at = TILES - 2 + step
        arrived(flag_z.at[step - 1], flag_send.at[at], flag_recv.at[at], z_peer(step))
        total = total + flag_z[step - 1]
    flag_own[2] = total
    at = TILES + NZ - 2
    send(flag_own.at[2], flag_core, flag_send.at[at], flag_recv.at[at], core_peer)
    z_round(p1_all, 16, 4, p1_sems, 4)
    arrived(flag_core, flag_send.at[at], flag_recv.at[at], core_peer)
    total = jnp.sum(total + flag_core[...], axis=0, keepdims=True)
    total = jnp.sum(total, axis=1, keepdims=True)
    flag_ref[...] = jnp.broadcast_to(total, (8, B))
    z_round(p1_all, 16, 4, p1_sems, 5)
    packets_arrived(1)
    settle[1].wait()
    second_index.wait()

    def second_row(i, carry):
        for c in range(NZ):
            for a in range(2):
                at = c * 2 + a
                for o in range(2):
                    rhs_q[at * B:(at + 1) * B, o * B:(o + 1) * B] = buf_s[inside(index_s[1, i * 4 + a * 2 + o, c], BLOCKS)]
        lhs = jnp.concatenate([p1_all[c * 16 + i * 2 + a] for c in range(NZ) for a in range(2)], axis=1)
        total = dot(lhs, rhs_q[...])
        q_part[0, i] = total[:, :B].astype(BF16)
        q_part[1, i] = total[:, B:].astype(BF16)
        return carry

    for h in range(4):
        z_round(p1_all, 16, 4, p1_sems, NZ - 2, (h,))
        lax.fori_loop(2 * h, 2 * h + 2, second_row, 0)
        rows = pl.ds(2 * h, 2)
        send(q_part.at[other, rows], q_in.at[rows], q_send.at[h], q_recv.at[h], core_peer)
    for h in range(4):
        rows = pl.ds(2 * h, 2)
        arrived(q_in.at[rows], q_send.at[h], q_recv.at[h], core_peer)
        both = q_part[layer, rows].astype(F32) + q_in[rows].astype(F32)
        q_ref[rows] = both.astype(BF16)
    for copy in sent:
        copy.wait_send()


def fast(f1_vals, f1_cols, p0_vals, p0_cols, s_vals, s_cols, p1_filter, q_filter):
    dma = pltpu.SemaphoreType.DMA
    vmem = pl.BlockSpec(memory_space=pltpu.VMEM)
    return pl.pallas_call(
        fast_kernel,
        out_shape=(
            jax.ShapeDtypeStruct((ROWS, 2, B, B), BF16),
            jax.ShapeDtypeStruct((ROWS, B, B), BF16),
            jax.ShapeDtypeStruct((8, B), F32),
        ),
        in_specs=[vmem] * 5 + [pl.BlockSpec(memory_space=pl.ANY)] * 3,
        out_specs=(vmem,) * 3,
        scratch_shapes=[
            pltpu.VMEM((PACKED, B, B), BF16),
            pltpu.VMEM((PACKED, B, B), BF16),
            pltpu.VMEM((BLOCKS, B, B), BF16),
            pltpu.VMEM((BLOCKS, B, B), BF16),
            pltpu.VMEM((2, 2, 3, CAP, B, B), BF16),
            pltpu.VMEM((2, 2, 2, HALF, B, B), BF16),
            pltpu.VMEM((NZ * 8, B, B), BF16),
            pltpu.VMEM((NZ * 16, B, B), BF16),
            pltpu.VMEM((NZ * B, 4 * B), BF16),
            pltpu.VMEM((NZ * 2 * B, 2 * B), BF16),
            pltpu.VMEM((2, ROWS, B, 2 * B), F32),
            pltpu.VMEM((ROWS, B, 2 * B), F32),
            pltpu.VMEM((2, ROWS, B, B), BF16),
            pltpu.VMEM((ROWS, B, B), BF16),
            pltpu.VMEM((8, B), I32),
            pltpu.VMEM((TILES, 8, B), I32),
            pltpu.VMEM((NZ, 8, B), I32),
            pltpu.VMEM((2, 8, B), I32),
            pltpu.VMEM((9, 8, B), I32),
            pltpu.VMEM((2, TILES, B), I32),
            pltpu.VMEM((2, 2, 3, TILES, B), I32),
            pltpu.VMEM((2, 32, B), I32),
            pltpu.VMEM((2, TILES, B), I32),
            pltpu.SMEM((2, 32, B), I32),
            pltpu.SMEM((2, TILES, B), I32),
            pltpu.VMEM((3, 8, B), F32),
            pltpu.VMEM((TILES - 1, 8, B), F32),
            pltpu.VMEM((NZ - 1, 8, B), F32),
            pltpu.VMEM((8, B), F32),
            dma((7,)),
            dma((TILES + NZ,)), dma((TILES + NZ,)),
            dma((2, 6)), dma((2, 6)),
            dma((2, 2, 2, 3)), dma((2, 2, 2, 3)),
            dma((2, 2, 5)), dma((2, 2, 5)),
            dma((2, 2, 2)), dma((2, 2, 2)),
            dma((4, NZ - 1)), dma((4, NZ - 1)),
            dma((ROWS,)), dma((ROWS,)),
            dma((4, NZ - 1)), dma((4, NZ - 1)),
            dma((4,)), dma((4,)),
            dma((TILES + NZ - 1,)), dma((TILES + NZ - 1,)),
            dma((4,)),
        ],
        compiler_params=pltpu.CompilerParams(
            collective_id=0, has_side_effects=True, vmem_limit_bytes=56 * 1024 * 1024
        ),
    )(
        f1_cols.T, p0_cols.T, s_cols.T, p1_filter.T, q_filter.T,
        f1_vals.reshape(ROWS, B, B),
        p0_vals.reshape(16, B, B),
        s_vals.reshape(16, B, B),
    )


ZERO = TILES * 16
F1C, P0C, SC, P1F, QF = 0, 1, 3, 5, 7


def dense_kernel(
    meta_ref, f1_ref, p0_ref, s_ref, p1_ref, q_ref,
    pan, span, f1_all, p1_all, rhs, rhs_q, part, part_in, q_part, q_in,
    meta_row, meta_z, meta_core, row_s, z_s, core_s,
    local_sem, meta_send, meta_recv, pan_send, pan_recv, f1_send, f1_recv,
    part_send, part_recv, p1_send, p1_recv, q_send, q_recv, smem_sem,
):
    r = lax.axis_index("row")
    u = lax.axis_index("col")
    layer = lax.axis_index("layer")
    x, y = r % SIDE, r // SIDE
    other = 1 - layer

    def chip(y_at, x_at):
        return (y_at % SIDE) * SIDE + x_at % SIDE

    own = [
        pltpu.make_async_copy(p0_ref, pan.at[pl.ds(r * 16, 16)], local_sem.at[0]),
        pltpu.make_async_copy(f1_ref, f1_all.at[pl.ds(u * 8, 8)], local_sem.at[1]),
        pltpu.make_async_copy(s_ref, span.at[pl.ds(r * 16, 16)], local_sem.at[2]),
    ]
    for copy in own:
        copy.start()

    barrier = pltpu.get_barrier_semaphore()
    for step in range(1, TILES):
        pl.semaphore_signal(barrier, inc=1, device_id=((r + step) % TILES, u, layer), device_id_type=MESH)
    for step in range(1, NZ):
        pl.semaphore_signal(barrier, inc=1, device_id=(r, (u + step) % NZ, layer), device_id_type=MESH)
    pl.semaphore_signal(barrier, inc=1, device_id=(r, u, other), device_id_type=MESH)

    pan[ZERO] = jnp.zeros((B, B), jnp.bfloat16)
    span[ZERO] = jnp.zeros((B, B), jnp.bfloat16)
    meta_row[r] = meta_ref[...]
    meta_z[u] = meta_ref[...]
    meta_core[layer] = meta_ref[...]
    pl.semaphore_wait(barrier, TILES - 1 + NZ - 1 + 1)

    sent = []

    def send(src, dst, send_sem, recv_sem, device):
        copy = pltpu.make_async_remote_copy(
            src_ref=src, dst_ref=dst, send_sem=send_sem, recv_sem=recv_sem,
            device_id=device, device_id_type=MESH,
        )
        copy.start()
        sent.append(copy)

    def arrived(dst, send_sem, recv_sem, device):
        pltpu.make_async_remote_copy(
            src_ref=dst, dst_ref=dst, send_sem=send_sem, recv_sem=recv_sem,
            device_id=device, device_id_type=MESH,
        ).wait_recv()

    for step in range(1, TILES):
        send(meta_ref, meta_row.at[r], meta_send.at[step], meta_recv.at[step], ((r + step) % TILES, u, layer))
    for step in range(1, NZ):
        at = TILES + step
        send(meta_ref, meta_z.at[u], meta_send.at[at], meta_recv.at[at], (r, (u + step) % NZ, layer))
    send(meta_ref, meta_core.at[layer], meta_send.at[0], meta_recv.at[0], (r, u, other))

    ways = ((0, 1), (0, -1), (1, 1), (1, -1))

    def tile_of(q, along, across):
        first, d = ways[q]
        if first == 0:
            return chip(y - d * across, x - d * along)
        return chip(y - d * along, x - d * across)

    def target(q, phase):
        first, d = ways[q]
        if (first + phase) % 2 == 0:
            return (chip(y, x + d), u, layer)
        return (chip(y + d, x), u, layer)

    def piece(panel, q, along, across):
        return panel.at[pl.ds(tile_of(q, along, across) * 16 + q * 4, 4)]

    def panel_send(which, q, phase, step, j):
        panel = (pan, span)[which]
        at = step if phase == 0 else 3 + step * 4 + j
        part_of = piece(panel, q, step, 0) if phase == 0 else piece(panel, q, j, step)
        send(part_of, part_of, pan_send.at[which, q, at], pan_recv.at[which, q, at], target(q, phase))

    def panel_arrived(which, q, phase, step, j):
        panel = (pan, span)[which]
        at = step if phase == 0 else 3 + step * 4 + j
        part_of = piece(panel, q, step + 1, 0) if phase == 0 else piece(panel, q, j, step + 1)
        arrived(part_of, pan_send.at[which, q, at], pan_recv.at[which, q, at], target(q, phase))

    def panel_begin(which):
        for q in range(4):
            panel_send(which, q, 0, 0, 0)
        for q in range(4):
            panel_send(which, q, 1, 0, 0)

    def panel_round(which, n):
        for q in range(4):
            if n < 3:
                panel_arrived(which, q, 0, n, 0)
                if n < 2:
                    panel_send(which, q, 0, n + 1, 0)
                panel_send(which, q, 1, 0, n + 1)
            else:
                step, j = (n - 3) // 4, (n - 3) % 4
                panel_arrived(which, q, 1, step, j)
                if step < 2:
                    panel_send(which, q, 1, step + 1, j)

    def z_piece(array, width, pieces, e, step):
        d = 1 - 2 * (e % 2)
        size = width // pieces
        return array.at[pl.ds(((u - d * step) % NZ) * width + e * size, size)]

    def z_send(array, width, pieces, sems, e, step):
        d = 1 - 2 * (e % 2)
        part_of = z_piece(array, width, pieces, e, step)
        send(part_of, part_of, sems[0].at[e, step], sems[1].at[e, step], (r, (u + d) % NZ, layer))

    def z_round(array, width, pieces, sems, n):
        for e in range(pieces):
            d = 1 - 2 * (e % 2)
            part_of = z_piece(array, width, pieces, e, n + 1)
            arrived(part_of, sems[0].at[e, n], sems[1].at[e, n], (r, (u + d) % NZ, layer))
            if n + 1 < NZ - 1:
                z_send(array, width, pieces, sems, e, n + 1)

    own[0].wait()
    for q in range(4):
        panel_send(0, q, 0, 0, 0)
    own[1].wait()
    f1_sems, p1_sems = (f1_send, f1_recv), (p1_send, p1_recv)
    for e in range(2):
        z_send(f1_all, 8, 2, f1_sems, e, 0)
    for q in range(4):
        panel_send(0, q, 1, 0, 0)
    own[2].wait()

    for step in range(1, TILES):
        arrived(meta_row.at[(r - step) % TILES], meta_send.at[step], meta_recv.at[step], ((r + step) % TILES, u, layer))
    for step in range(1, NZ):
        at = TILES + step
        arrived(meta_z.at[(u - step) % NZ], meta_send.at[at], meta_recv.at[at], (r, (u + step) % NZ, layer))
    arrived(meta_core.at[other], meta_send.at[0], meta_recv.at[0], (r, u, other))
    tables = [
        pltpu.make_async_copy(meta_row, row_s, smem_sem.at[0]),
        pltpu.make_async_copy(meta_z, z_s, smem_sem.at[1]),
        pltpu.make_async_copy(meta_core, core_s, smem_sem.at[2]),
    ]
    for copy in tables:
        copy.start()

    for n in range(15):
        if n == 11:
            panel_begin(1)
        panel_round(0, n)
        if n < NZ - 1:
            z_round(f1_all, 8, 2, f1_sems, n)
    for copy in tables:
        copy.wait()

    def choose(panel, index):
        return panel[index]

    def first_row(i, carry):
        for c in range(NZ):
            k = z_s[c, i, F1C]
            t = lax.shift_right_logical(k, 4)
            base = t * 16 + c * 2
            n0, n1 = row_s[t, c, P0C], row_s[t, c, P0C + 1]
            for o in range(4):
                want = core_s[o // 2, i, P1F + o % 2]
                index = jnp.where(n0 == want, base, jnp.where(n1 == want, base + 1, ZERO))
                rhs[c * B:(c + 1) * B, o * B:(o + 1) * B] = choose(pan, index)
        lhs = jnp.concatenate([f1_all[c * 8 + i] for c in range(NZ)], axis=1)
        total = jnp.dot(lhs, rhs[...], preferred_element_type=jnp.float32)
        part[0, i] = total[:, :2 * B]
        part[1, i] = total[:, 2 * B:]
        return carry

    def part_send_row(i):
        send(part.at[other, i], part_in.at[i], part_send.at[i], part_recv.at[i], (r, u, other))

    for h in range(4):
        lax.fori_loop(2 * h, 2 * h + 2, first_row, 0)
        part_send_row(2 * h)
        part_send_row(2 * h + 1)
        if h < 3:
            panel_round(1, h)

    def finish_row(i, carry):
        total = (part[layer, i] + part_in[i]).astype(jnp.bfloat16)
        for o in range(2):
            block = total[:, o * B:(o + 1) * B]
            p1_all[u * 16 + i * 2 + o] = block
            p1_ref[i, o] = block
        return carry

    for e in range(4):
        for i in (2 * e, 2 * e + 1):
            arrived(part_in.at[i], part_send.at[i], part_recv.at[i], (r, u, other))
        lax.fori_loop(2 * e, 2 * e + 2, finish_row, 0)
        z_send(p1_all, 16, 4, p1_sems, e, 0)

    for n in range(12):
        panel_round(1, n + 3)
        if n < NZ - 1:
            z_round(p1_all, 16, 4, p1_sems, n)

    def second_row(i, carry):
        for c in range(NZ):
            for a in range(2):
                k = z_s[c, i, P1F + a]
                t = lax.shift_right_logical(k, 4)
                base = t * 16 + c * 2
                n0, n1 = row_s[t, c, SC], row_s[t, c, SC + 1]
                at = c * 2 + a
                for o in range(2):
                    want = core_s[o, i, QF]
                    index = jnp.where(n0 == want, base, jnp.where(n1 == want, base + 1, ZERO))
                    rhs_q[at * B:(at + 1) * B, o * B:(o + 1) * B] = choose(span, index)
        lhs = jnp.concatenate([p1_all[c * 16 + i * 2 + a] for c in range(NZ) for a in range(2)], axis=1)
        total = jnp.dot(lhs, rhs_q[...], preferred_element_type=jnp.float32)
        q_part[0, i] = total[:, :B].astype(jnp.bfloat16)
        q_part[1, i] = total[:, B:].astype(jnp.bfloat16)
        return carry

    for h in range(2):
        lax.fori_loop(4 * h, 4 * h + 4, second_row, 0)
        rows = pl.ds(4 * h, 4)
        send(q_part.at[other, rows], q_in.at[rows], q_send.at[h], q_recv.at[h], (r, u, other))
    for h in range(2):
        rows = pl.ds(4 * h, 4)
        arrived(q_in.at[rows], q_send.at[h], q_recv.at[h], (r, u, other))
        both = q_part[layer, rows].astype(jnp.float32) + q_in[rows].astype(jnp.float32)
        q_ref[rows] = both.astype(jnp.bfloat16)
    for copy in sent:
        copy.wait_send()


def dense(f1_vals, f1_cols, p0_vals, p0_cols, s_vals, s_cols, p1_filter, q_filter):
    meta = jnp.concatenate([f1_cols, p0_cols, s_cols, p1_filter, q_filter], axis=1)
    meta = jnp.pad(meta, ((0, 0), (0, B - meta.shape[1])))
    bf16, f32, i32 = jnp.bfloat16, jnp.float32, jnp.int32
    dma = pltpu.SemaphoreType.DMA
    p1, q = pl.pallas_call(
        dense_kernel,
        out_shape=(
            jax.ShapeDtypeStruct((ROWS, 2, B, B), bf16),
            jax.ShapeDtypeStruct((ROWS, B, B), bf16),
        ),
        in_specs=[pl.BlockSpec(memory_space=pltpu.VMEM)] + [pl.BlockSpec(memory_space=pl.ANY)] * 3,
        out_specs=(pl.BlockSpec(memory_space=pltpu.VMEM),) * 2,
        scratch_shapes=[
            pltpu.VMEM((TILES * 16 + 1, B, B), bf16),
            pltpu.VMEM((TILES * 16 + 1, B, B), bf16),
            pltpu.VMEM((NZ * 8, B, B), bf16),
            pltpu.VMEM((NZ * 16, B, B), bf16),
            pltpu.VMEM((NZ * B, 4 * B), bf16),
            pltpu.VMEM((NZ * 2 * B, 2 * B), bf16),
            pltpu.VMEM((2, ROWS, B, 2 * B), f32),
            pltpu.VMEM((ROWS, B, 2 * B), f32),
            pltpu.VMEM((2, ROWS, B, B), bf16),
            pltpu.VMEM((ROWS, B, B), bf16),
            pltpu.VMEM((TILES, 8, B), i32),
            pltpu.VMEM((NZ, 8, B), i32),
            pltpu.VMEM((2, 8, B), i32),
            pltpu.SMEM((TILES, 8, B), i32),
            pltpu.SMEM((NZ, 8, B), i32),
            pltpu.SMEM((2, 8, B), i32),
            dma((3,)),
            dma((TILES + NZ,)), dma((TILES + NZ,)),
            dma((2, 4, 15)), dma((2, 4, 15)),
            dma((2, NZ - 1)), dma((2, NZ - 1)),
            dma((ROWS,)), dma((ROWS,)),
            dma((4, NZ - 1)), dma((4, NZ - 1)),
            dma((2,)), dma((2,)),
            dma((3,)),
        ],
        compiler_params=pltpu.CompilerParams(
            collective_id=1, has_side_effects=True, vmem_limit_bytes=56 * 1024 * 1024
        ),
    )(
        meta,
        f1_vals.reshape(ROWS, B, B),
        p0_vals.reshape(16, B, B),
        s_vals.reshape(16, B, B),
    )
    return p1, q.reshape(ROWS, 1, B, B)


def body(*args):
    p1, q, flag = fast(*args)
    return lax.cond(
        flag[0, 0] > 0.5,
        lambda p1, q, *args: dense(*args),
        lambda p1, q, *args: (p1, q),
        p1, q.reshape(ROWS, 1, B, B), *args,
    )


def solution(mesh):
    return jax.shard_map(
        body,
        mesh=mesh,
        in_specs=(
            P("row", ("col", "layer"), None, None),
            P("row", ("col", "layer")),
            P(("row", "layer"), "col", None, None),
            P(("row", "layer"), "col"),
            P(("row", "layer"), "col", None, None),
            P(("row", "layer"), "col"),
            P("row", ("col", "layer")),
            P("row", ("col", "layer")),
        ),
        out_specs=(P("row", ("col", "layer"), None, None), P("row", ("col", "layer"), None, None)),
        check_vma=False,
    )
```

```python
import jax
import jax.numpy as jnp
from jax import lax
from jax.experimental import pallas as pl
from jax.experimental.pallas import tpu as pltpu
from jax.sharding import PartitionSpec as P

MESH = pl.DeviceIdType.MESH
B = 128
SIDE = 4
NZ = 8
ROWS = 8
TILES = SIDE * SIDE
CAP = 12
HALF = CAP // 2
PACKED = 65
BLOCKS = PACKED + 6 * CAP
F32, I32, BF16 = jnp.float32, jnp.int32, jnp.bfloat16


def inside(index, count):
    return lax.max(lax.min(index, count - 1), 0)


def fast_kernel(
    f1c_ref, p0c_ref, sc_ref, p1f_ref, qf_ref, f1_ref, p0_ref, s_ref, p1_ref, q_ref, flag_ref,
    whole_p, whole_s, buf_p, buf_s, outs, relays, f1_all, p1_all, rhs, rhs_q, part, part_in, q_part, q_in,
    own_tile, row_tiles, z_tiles, core_tiles, demand, code, code_in, index_v, list_v, index_s, list_s,
    flag_own, flag_row, flag_z, flag_core,
    local_sem, meta_send, meta_recv, code_send, code_recv, pan_send, pan_recv, pack_send, pack_recv,
    rel_send, rel_recv, f1_send, f1_recv, part_send, part_recv, p1_send, p1_recv, q_send, q_recv,
    flag_send, flag_recv, smem_sem,
):
    r = lax.axis_index("row")
    u = lax.axis_index("col")
    layer = lax.axis_index("layer")
    x, y = r % SIDE, r // SIDE
    other = 1 - layer
    whole, bufs = (whole_p, whole_s), (buf_p, buf_s)

    def chip(y_at, x_at):
        return ((y_at % SIDE) * SIDE + x_at % SIDE, u, layer)

    own = []
    for which, ref in ((0, p0_ref), (1, s_ref)):
        own.append(pltpu.make_async_copy(ref.at[pl.ds(0, 8)], whole[which].at[pl.ds(1 + x * 8, 8)], local_sem.at[2 * which]))
        own.append(pltpu.make_async_copy(ref.at[pl.ds(8, 8)], whole[which].at[pl.ds(33 + y * 8, 8)], local_sem.at[2 * which + 1]))
    own.append(pltpu.make_async_copy(f1_ref, f1_all.at[pl.ds(u * 8, 8)], local_sem.at[4]))
    for copy in own:
        copy.start()

    barrier = pltpu.get_barrier_semaphore()
    for step in range(1, TILES):
        pl.semaphore_signal(barrier, inc=1, device_id=((r + step) % TILES, u, layer), device_id_type=MESH)
    for step in range(1, NZ):
        pl.semaphore_signal(barrier, inc=1, device_id=(r, (u + step) % NZ, layer), device_id_type=MESH)
    pl.semaphore_signal(barrier, inc=1, device_id=(r, u, other), device_id_type=MESH)

    for panel in whole:
        panel[0] = jnp.zeros((B, B), BF16)
    sub8 = lax.broadcasted_iota(I32, (8, B), 0)
    lane8 = lax.broadcasted_iota(I32, (8, B), 1)

    own_tile[...] = jnp.full((8, B), -1, I32)
    for at, ref in ((0, p0c_ref), (2, sc_ref), (4, f1c_ref), (5, p1f_ref), (7, qf_ref)):
        own_tile[at:at + ref.shape[0], 0:8] = ref[...]
    row_tiles[r] = own_tile[...]
    z_tiles[u] = own_tile[...]
    core_tiles[layer] = own_tile[...]
    pl.semaphore_wait(barrier, TILES - 1 + NZ - 1 + 1)

    sent = []

    def remote(src, dst, send_sem, recv_sem, device):
        return pltpu.make_async_remote_copy(
            src_ref=src, dst_ref=dst, send_sem=send_sem, recv_sem=recv_sem,
            device_id=device, device_id_type=MESH,
        )

    def send(src, dst, send_sem, recv_sem, device):
        copy = remote(src, dst, send_sem, recv_sem, device)
        copy.start()
        sent.append(copy)

    def arrived(dst, send_sem, recv_sem, device):
        remote(dst, dst, send_sem, recv_sem, device).wait_recv()

    def row_peer(step):
        return ((r + step) % TILES, u, layer)

    def z_peer(step):
        return (r, (u + step) % NZ, layer)

    core_peer = (r, u, other)

    for step in range(1, NZ):
        at = TILES + step
        send(own_tile, z_tiles.at[u], meta_send.at[at], meta_recv.at[at], z_peer(step))
    send(own_tile, core_tiles.at[layer], meta_send.at[0], meta_recv.at[0], core_peer)
    for step in range(1, TILES):
        send(own_tile, row_tiles.at[r], meta_send.at[step], meta_recv.at[step], row_peer(step))

    def along(axis, d):
        return chip(y, x + d) if axis == 0 else chip(y + d, x)

    def quarter(which, h, q, d):
        at = (x if h == 0 else y) - d
        return whole[which].at[pl.ds(1 + 32 * h + (at % SIDE) * 8 + q * 4, 4)]

    def panel_begin(which):
        for n in range(2):
            for h in range(2):
                for way in (0, 1):
                    q, d = n if way == 0 else 1 - n, 1 - 2 * way
                    part_of = quarter(which, h, q, 0)
                    send(part_of, part_of, pan_send.at[which, h, way, n], pan_recv.at[which, h, way, n], along(h, d))

    def panel_round(which, n):
        for h in range(2):
            for way in (0, 1):
                d = 1 - 2 * way
                q = (n if way == 0 else 1 - n) if n < 2 else way
                part_of = quarter(which, h, q, d if n < 2 else 2 * d)
                arrived(part_of, pan_send.at[which, h, way, n], pan_recv.at[which, h, way, n], along(h, d))
                if n == 0:
                    send(part_of, part_of, pan_send.at[which, h, way, 2], pan_recv.at[which, h, way, 2], along(h, d))

    def packet(which, h, d):
        return bufs[which].at[pl.ds(PACKED + (h * 3 + d - 1) * CAP, CAP)]

    def half_of(ref, e):
        return ref.at[pl.ds(e * HALF, HALF)]

    def relay(which):
        for h in range(2):
            for e, way in ((0, 1), (1, -1)):
                arrived(relays.at[which, h, e], rel_send.at[which, h, e], rel_recv.at[which, h, e], along(1 - h, way))
                send(
                    relays.at[which, h, e], half_of(packet(which, h, 2), e),
                    pack_send.at[which, h, 3 + e], pack_recv.at[which, h, 3 + e], along(1 - h, way),
                )

    def packets_arrived(which):
        for h in range(2):
            for d in (1, 3):
                arrived(packet(which, h, d), pack_send.at[which, h, d - 1], pack_recv.at[which, h, d - 1], along(1 - h, 1))
            for e in range(2):
                arrived(half_of(packet(which, h, 2), e), pack_send.at[which, h, 3 + e], pack_recv.at[which, h, 3 + e], along(1 - h, 1))

    def z_piece(array, width, pieces, e, step):
        d = 1 - 2 * (e % 2)
        size = width // pieces
        return array.at[pl.ds(((u - d * step) % NZ) * width + e * size, size)]

    def z_send(array, width, pieces, sems, e, step):
        d = 1 - 2 * (e % 2)
        part_of = z_piece(array, width, pieces, e, step)
        send(part_of, part_of, sems[0].at[e, step], sems[1].at[e, step], z_peer(d))

    def z_round(array, width, pieces, sems, n, only=None):
        for e in range(pieces) if only is None else only:
            d = 1 - 2 * (e % 2)
            arrived(z_piece(array, width, pieces, e, n + 1), sems[0].at[e, n], sems[1].at[e, n], z_peer(d))
            if n + 1 < NZ - 1:
                z_send(array, width, pieces, sems, e, n + 1)

    f1_sems, p1_sems = (f1_send, f1_recv), (p1_send, p1_recv)
    own[0].wait()
    own[1].wait()
    panel_begin(0)
    own[4].wait()
    for e in range(4):
        z_send(f1_all, 8, 4, f1_sems, e, 0)
    own[2].wait()
    own[3].wait()

    for step in range(1, NZ):
        at = TILES + step
        arrived(z_tiles.at[(u - step) % NZ], meta_send.at[at], meta_recv.at[at], z_peer(step))
    arrived(core_tiles.at[other], meta_send.at[0], meta_recv.at[0], core_peer)

    def column_of(line):
        spread = jnp.where(sub8 == lane8, jnp.broadcast_to(line.astype(F32), (8, B)), 0.0)
        return jnp.broadcast_to(jnp.sum(spread, axis=1, keepdims=True), (8, B))

    for at in range(3):
        merged = jnp.zeros((8, B), F32)
        for c in range(NZ):
            merged = jnp.where(lane8 == c, column_of(z_tiles[c, 4 + at:5 + at, :]), merged)
        demand[at] = merged.astype(I32)
    for o in range(4):
        demand[3 + o] = column_of(core_tiles[o // 2, 5 + o % 2:6 + o % 2, :]).astype(I32)
    for o in range(2):
        demand[7 + o] = column_of(core_tiles[o, 7:8, :]).astype(I32)

    for step in range(1, TILES):
        arrived(row_tiles.at[(r - step) % TILES], meta_send.at[step], meta_recv.at[step], row_peer(step))

    tile = lax.broadcasted_iota(I32, (TILES, B), 0)
    lane = lax.broadcasted_iota(I32, (TILES, B), 1)
    tile_y, tile_x = lax.shift_right_logical(tile, 2), tile & 3
    upper = lane >= 4
    lane_a = lax.broadcasted_iota(I32, (B, B), 0)
    lane_b = lax.broadcasted_iota(I32, (B, B), 1)
    same = lax.shift_right_logical(lane_a, 2) == lax.shift_right_logical(lane_b, 2)
    one, nil = jnp.ones((), F32), jnp.zeros((), F32)
    lanes_all = jnp.where(same, one, nil)
    lanes_before = jnp.where(same & (lane_a < lane_b), one, nil)
    tile_a = lax.broadcasted_iota(I32, (TILES, TILES), 0)
    tile_b = lax.broadcasted_iota(I32, (TILES, TILES), 1)
    before = tile_b < tile_a
    same_y = lax.shift_right_logical(tile_a, 2) == lax.shift_right_logical(tile_b, 2)
    same_x = (tile_a & 3) == (tile_b & 3)
    tiles_y = jnp.where(before & same_y, one, nil)
    tiles_x = jnp.where(before & same_x, one, nil)

    def dot(a, b):
        return jnp.dot(a, b, preferred_element_type=F32)

    name = [[row_tiles[:, 2 * which + w, :] for w in range(2)] for which in range(2)]

    def wide(at, i):
        return jnp.broadcast_to(demand[at, i:i + 1, :], (TILES, B))

    def matches(which):
        result = []
        for i in range(ROWS):
            wants = [wide(at, i) for at in (range(3, 7) if which == 0 else range(7, 9))]
            for at in (range(1) if which == 0 else range(1, 3)):
                hit = lax.shift_right_logical(wide(at, i), 4) == tile
                result.append([[hit & (name[which][w] == want) for w in range(2)] for want in wants])
        return result

    def needs(masks):
        total = []
        for w in range(2):
            need = masks[0][0][w]
            for row in masks:
                for slot in row:
                    need = need | slot[w]
            total.append(jnp.where(need, one, nil))
        return total

    def ranks(need):
        both = need[0] + need[1]
        all_of = dot(both, lanes_all)
        first = jnp.where(upper, dot(tiles_x, all_of), dot(tiles_y, all_of)) + dot(both, lanes_before)
        return [first, first + need[0]]

    within = (lane & 3) * 2
    place = 1 + jnp.where(upper, 32 + tile_y * 8 + within, tile_x * 8 + within)
    offset = jnp.where(upper, tile_x - x, tile_y - y) & 3
    here = offset == 0
    packed = PACKED + jnp.where(upper, 3 * CAP, 0) + (offset - 1) * CAP
    place_f, packed_f = place.astype(F32), packed.astype(F32)

    def own_code(which):
        masks = matches(which)
        need = needs(masks)
        rank = ranks(need)
        code[which] = (jnp.where(need[0] > 0.5, rank[0] + 1.0, 0.0) + 64.0 * jnp.where(need[1] > 0.5, rank[1] + 1.0, 0.0)).astype(I32)
        for axis in range(2):
            for d in (1, 2, 3):
                at = axis * 3 + d - 1
                send(
                    code.at[which], code_in.at[which, axis, 3 - d],
                    code_send.at[which, at], code_recv.at[which, axis * 3 + 3 - d], along(axis, d),
                )
        return masks, need, rank

    def own_index(which, masks, need, rank):
        spot, worst = [], jnp.zeros((TILES, B), F32)
        for w in range(2):
            fits = rank[w] < float(CAP)
            spot.append(jnp.where(here, place_f + float(w), jnp.where(fits, packed_f + rank[w], 0.0)))
            worst = worst + jnp.where((need[w] > 0.5) & jnp.logical_not(fits | here), one, nil)
        at = 0
        for row in masks:
            for slot in row:
                chosen = jnp.where(slot[0], spot[0], jnp.where(slot[1], spot[1], 0.0))
                line = jnp.sum(chosen, axis=0, keepdims=True)
                index_v[which, at:at + 1, :] = line.astype(I32)
                at += 1
        return worst

    def peer_lists(which):
        table = jnp.zeros((TILES, B), F32)
        for h in range(2):
            axis = 1 - h
            mine = (jnp.logical_not(upper) & (tile_y == y)) if h == 0 else (upper & (lane < 8) & (tile_x == x))
            for d in (1, 2, 3):
                at = axis * 3 + d - 1
                arrived(code_in.at[which, axis, d - 1], code_send.at[which, at], code_recv.at[which, at], along(axis, d))
                there = jnp.where(mine, code_in[which, axis, d - 1], 0)
                rank = [there & 63, lax.shift_right_logical(there, 6)]
                slots = jnp.zeros((TILES, B), F32)
                for j in range(CAP):
                    chosen = jnp.where(rank[0] == j + 1, place_f, 0.0) + jnp.where(rank[1] == j + 1, place_f + 1.0, 0.0)
                    line = jnp.sum(chosen, axis=0, keepdims=True)
                    slots = jnp.where(tile == j, jnp.broadcast_to(line, (TILES, B)), slots)
                column = jnp.broadcast_to(jnp.sum(slots, axis=1, keepdims=True), (TILES, B))
                table = jnp.where(lane == (which * 2 + h) * 3 + d - 1, column, table)
        return table

    found = own_code(0)
    panel_round(0, 0)
    z_round(f1_all, 8, 4, f1_sems, 0)
    lists = [pltpu.make_async_copy(list_v.at[w], list_s.at[w], smem_sem.at[w]) for w in range(2)]
    list_v[0] = peer_lists(0).astype(I32)
    lists[0].start()
    z_round(f1_all, 8, 4, f1_sems, 1)
    panel_round(0, 1)
    panel_round(0, 2)
    settle = [pltpu.make_async_copy(whole[w], bufs[w].at[pl.ds(0, PACKED)], local_sem.at[5 + w]) for w in range(2)]
    z_round(f1_all, 8, 4, f1_sems, 2)
    lists[0].wait()

    def pack(which, ref):
        for h in range(2):
            for d in (2, 1, 3):
                column = (which * 2 + h) * 3 + d - 1
                for j in range(CAP):
                    outs[which, h, d - 1, j] = whole[which][inside(ref[j, column], PACKED)]
                axis = 1 - h
                if d == 2:
                    for e, way in ((0, 1), (1, -1)):
                        send(
                            half_of(outs.at[which, h, 1], e), relays.at[which, h, e],
                            rel_send.at[which, h, e], rel_recv.at[which, h, e], along(axis, way),
                        )
                else:
                    way = 1 if d == 1 else -1
                    send(
                        outs.at[which, h, d - 1], packet(which, h, 4 - d),
                        pack_send.at[which, h, d - 1], pack_recv.at[which, h, 3 - d], along(axis, way),
                    )

    pack(0, list_s.at[0])
    settle[0].start()
    found_s = own_code(1)
    z_round(f1_all, 8, 4, f1_sems, 3)
    over = own_index(0, *found)
    first_index = pltpu.make_async_copy(index_v.at[0], index_s.at[0], smem_sem.at[2])
    first_index.start()
    z_round(f1_all, 8, 4, f1_sems, 4)
    relay(0)
    panel_begin(1)
    z_round(f1_all, 8, 4, f1_sems, 5)
    list_v[1] = peer_lists(1).astype(I32)
    lists[1].start()
    over = over + own_index(1, *found_s)
    second_index = pltpu.make_async_copy(index_v.at[1], index_s.at[1], smem_sem.at[3])
    second_index.start()
    flag_own[0] = over[:8] + over[8:]
    z_round(f1_all, 8, 4, f1_sems, 6)
    first_index.wait()
    settle[0].wait()
    packets_arrived(0)
    lists[1].wait()

    def first_row(i, carry):
        for c in range(NZ):
            for o in range(4):
                rhs[c * B:(c + 1) * B, o * B:(o + 1) * B] = buf_p[inside(index_s[0, i * 4 + o, c], BLOCKS)]
        lhs = jnp.concatenate([f1_all[c * 8 + i] for c in range(NZ)], axis=1)
        total = dot(lhs, rhs[...])
        part[0, i] = total[:, :2 * B]
        part[1, i] = total[:, 2 * B:]
        return carry

    def part_send_row(i):
        send(part.at[other, i], part_in.at[i], part_send.at[i], part_recv.at[i], core_peer)

    def finish_row(i, carry):
        total = (part[layer, i] + part_in[i]).astype(BF16)
        for o in range(2):
            block = total[:, o * B:(o + 1) * B]
            p1_all[u * 16 + i * 2 + o] = block
            p1_ref[i, o] = block
        return carry

    def finish(e):
        for i in (2 * e, 2 * e + 1):
            arrived(part_in.at[i], part_send.at[i], part_recv.at[i], core_peer)
        lax.fori_loop(2 * e, 2 * e + 2, finish_row, 0)
        z_send(p1_all, 16, 4, p1_sems, e, 0)

    for h in range(4):
        lax.fori_loop(2 * h, 2 * h + 2, first_row, 0)
        part_send_row(2 * h)
        part_send_row(2 * h + 1)
        if h > 0:
            finish(h - 1)
        if h == 2:
            panel_round(1, 0)
    finish(3)

    for step in range(1, TILES):
        send(flag_own.at[0], flag_row.at[step - 1], flag_send.at[step - 1], flag_recv.at[step - 1], row_peer(step))
    z_round(p1_all, 16, 4, p1_sems, 0)
    panel_round(1, 1)
    panel_round(1, 2)
    pack(1, list_s.at[1])
    settle[1].start()
    z_round(p1_all, 16, 4, p1_sems, 1)
    total = flag_own[0]
    for step in range(1, TILES):
        arrived(flag_row.at[step - 1], flag_send.at[step - 1], flag_recv.at[step - 1], row_peer(step))
        total = total + flag_row[step - 1]
    flag_own[1] = total
    for step in range(1, NZ):
        at = TILES - 2 + step
        send(flag_own.at[1], flag_z.at[step - 1], flag_send.at[at], flag_recv.at[at], z_peer(step))
    z_round(p1_all, 16, 4, p1_sems, 2)
    relay(1)
    z_round(p1_all, 16, 4, p1_sems, 3)
    for step in range(1, NZ):
        at = TILES - 2 + step
        arrived(flag_z.at[step - 1], flag_send.at[at], flag_recv.at[at], z_peer(step))
        total = total + flag_z[step - 1]
    flag_own[2] = total
    at = TILES + NZ - 2
    send(flag_own.at[2], flag_core, flag_send.at[at], flag_recv.at[at], core_peer)
    z_round(p1_all, 16, 4, p1_sems, 4)
    arrived(flag_core, flag_send.at[at], flag_recv.at[at], core_peer)
    total = total + flag_core[...]
    flag_ref[0, 0] = jnp.where(jnp.sum(total) > 0.5, 1, 0)
    z_round(p1_all, 16, 4, p1_sems, 5)
    packets_arrived(1)
    settle[1].wait()
    second_index.wait()

    def second_row(i, carry):
        for c in range(NZ):
            for a in range(2):
                at = c * 2 + a
                for o in range(2):
                    rhs_q[at * B:(at + 1) * B, o * B:(o + 1) * B] = buf_s[inside(index_s[1, i * 4 + a * 2 + o, c], BLOCKS)]
        lhs = jnp.concatenate([p1_all[c * 16 + i * 2 + a] for c in range(NZ) for a in range(2)], axis=1)
        total = dot(lhs, rhs_q[...])
        q_part[0, i] = total[:, :B].astype(BF16)
        q_part[1, i] = total[:, B:].astype(BF16)
        return carry

    for h in range(4):
        z_round(p1_all, 16, 4, p1_sems, NZ - 2, (h,))
        lax.fori_loop(2 * h, 2 * h + 2, second_row, 0)
        rows = pl.ds(2 * h, 2)
        send(q_part.at[other, rows], q_in.at[rows], q_send.at[h], q_recv.at[h], core_peer)
    for h in range(4):
        rows = pl.ds(2 * h, 2)
        arrived(q_in.at[rows], q_send.at[h], q_recv.at[h], core_peer)
        both = q_part[layer, rows].astype(F32) + q_in[rows].astype(F32)
        q_ref[rows] = both.astype(BF16)
    for copy in sent:
        copy.wait_send()


def fast(f1_vals, f1_cols, p0_vals, p0_cols, s_vals, s_cols, p1_filter, q_filter):
    dma = pltpu.SemaphoreType.DMA
    vmem = pl.BlockSpec(memory_space=pltpu.VMEM)
    return pl.pallas_call(
        fast_kernel,
        out_shape=(
            jax.ShapeDtypeStruct((ROWS, 2, B, B), BF16),
            jax.ShapeDtypeStruct((ROWS, B, B), BF16),
            jax.ShapeDtypeStruct((1, 1), I32),
        ),
        in_specs=[vmem] * 5 + [pl.BlockSpec(memory_space=pl.ANY)] * 3,
        out_specs=(vmem, vmem, pl.BlockSpec(memory_space=pltpu.SMEM)),
        scratch_shapes=[
            pltpu.VMEM((PACKED, B, B), BF16),
            pltpu.VMEM((PACKED, B, B), BF16),
            pltpu.VMEM((BLOCKS, B, B), BF16),
            pltpu.VMEM((BLOCKS, B, B), BF16),
            pltpu.VMEM((2, 2, 3, CAP, B, B), BF16),
            pltpu.VMEM((2, 2, 2, HALF, B, B), BF16),
            pltpu.VMEM((NZ * 8, B, B), BF16),
            pltpu.VMEM((NZ * 16, B, B), BF16),
            pltpu.VMEM((NZ * B, 4 * B), BF16),
            pltpu.VMEM((NZ * 2 * B, 2 * B), BF16),
            pltpu.VMEM((2, ROWS, B, 2 * B), F32),
            pltpu.VMEM((ROWS, B, 2 * B), F32),
            pltpu.VMEM((2, ROWS, B, B), BF16),
            pltpu.VMEM((ROWS, B, B), BF16),
            pltpu.VMEM((8, B), I32),
            pltpu.VMEM((TILES, 8, B), I32),
            pltpu.VMEM((NZ, 8, B), I32),
            pltpu.VMEM((2, 8, B), I32),
            pltpu.VMEM((9, 8, B), I32),
            pltpu.VMEM((2, TILES, B), I32),
            pltpu.VMEM((2, 2, 3, TILES, B), I32),
            pltpu.VMEM((2, 32, B), I32),
            pltpu.VMEM((2, TILES, B), I32),
            pltpu.SMEM((2, 32, B), I32),
            pltpu.SMEM((2, TILES, B), I32),
            pltpu.VMEM((3, 8, B), F32),
            pltpu.VMEM((TILES - 1, 8, B), F32),
            pltpu.VMEM((NZ - 1, 8, B), F32),
            pltpu.VMEM((8, B), F32),
            dma((7,)),
            dma((TILES + NZ,)), dma((TILES + NZ,)),
            dma((2, 6)), dma((2, 6)),
            dma((2, 2, 2, 3)), dma((2, 2, 2, 3)),
            dma((2, 2, 5)), dma((2, 2, 5)),
            dma((2, 2, 2)), dma((2, 2, 2)),
            dma((4, NZ - 1)), dma((4, NZ - 1)),
            dma((ROWS,)), dma((ROWS,)),
            dma((4, NZ - 1)), dma((4, NZ - 1)),
            dma((4,)), dma((4,)),
            dma((TILES + NZ - 1,)), dma((TILES + NZ - 1,)),
            dma((4,)),
        ],
        compiler_params=pltpu.CompilerParams(
            collective_id=0, has_side_effects=True, vmem_limit_bytes=56 * 1024 * 1024
        ),
    )(
        f1_cols.T, p0_cols.T, s_cols.T, p1_filter.T, q_filter.T,
        f1_vals.reshape(ROWS, B, B),
        p0_vals.reshape(16, B, B),
        s_vals.reshape(16, B, B),
    )


ZERO = TILES * 16
F1C, P0C, SC, P1F, QF = 0, 1, 3, 5, 7


def dense_kernel(
    meta_ref, f1_ref, p0_ref, s_ref, p1_ref, q_ref,
    pan, span, f1_all, p1_all, rhs, rhs_q, part, part_in, q_part, q_in,
    meta_row, meta_z, meta_core, row_s, z_s, core_s,
    local_sem, meta_send, meta_recv, pan_send, pan_recv, f1_send, f1_recv,
    part_send, part_recv, p1_send, p1_recv, q_send, q_recv, smem_sem,
):
    r = lax.axis_index("row")
    u = lax.axis_index("col")
    layer = lax.axis_index("layer")
    x, y = r % SIDE, r // SIDE
    other = 1 - layer

    def chip(y_at, x_at):
        return (y_at % SIDE) * SIDE + x_at % SIDE

    own = [
        pltpu.make_async_copy(p0_ref, pan.at[pl.ds(r * 16, 16)], local_sem.at[0]),
        pltpu.make_async_copy(f1_ref, f1_all.at[pl.ds(u * 8, 8)], local_sem.at[1]),
        pltpu.make_async_copy(s_ref, span.at[pl.ds(r * 16, 16)], local_sem.at[2]),
    ]
    for copy in own:
        copy.start()

    barrier = pltpu.get_barrier_semaphore()
    for step in range(1, TILES):
        pl.semaphore_signal(barrier, inc=1, device_id=((r + step) % TILES, u, layer), device_id_type=MESH)
    for step in range(1, NZ):
        pl.semaphore_signal(barrier, inc=1, device_id=(r, (u + step) % NZ, layer), device_id_type=MESH)
    pl.semaphore_signal(barrier, inc=1, device_id=(r, u, other), device_id_type=MESH)

    pan[ZERO] = jnp.zeros((B, B), jnp.bfloat16)
    span[ZERO] = jnp.zeros((B, B), jnp.bfloat16)
    meta_row[r] = meta_ref[...]
    meta_z[u] = meta_ref[...]
    meta_core[layer] = meta_ref[...]
    pl.semaphore_wait(barrier, TILES - 1 + NZ - 1 + 1)

    sent = []

    def send(src, dst, send_sem, recv_sem, device):
        copy = pltpu.make_async_remote_copy(
            src_ref=src, dst_ref=dst, send_sem=send_sem, recv_sem=recv_sem,
            device_id=device, device_id_type=MESH,
        )
        copy.start()
        sent.append(copy)

    def arrived(dst, send_sem, recv_sem, device):
        pltpu.make_async_remote_copy(
            src_ref=dst, dst_ref=dst, send_sem=send_sem, recv_sem=recv_sem,
            device_id=device, device_id_type=MESH,
        ).wait_recv()

    for step in range(1, TILES):
        send(meta_ref, meta_row.at[r], meta_send.at[step], meta_recv.at[step], ((r + step) % TILES, u, layer))
    for step in range(1, NZ):
        at = TILES + step
        send(meta_ref, meta_z.at[u], meta_send.at[at], meta_recv.at[at], (r, (u + step) % NZ, layer))
    send(meta_ref, meta_core.at[layer], meta_send.at[0], meta_recv.at[0], (r, u, other))

    ways = ((0, 1), (0, -1), (1, 1), (1, -1))

    def tile_of(q, along, across):
        first, d = ways[q]
        if first == 0:
            return chip(y - d * across, x - d * along)
        return chip(y - d * along, x - d * across)

    def target(q, phase):
        first, d = ways[q]
        if (first + phase) % 2 == 0:
            return (chip(y, x + d), u, layer)
        return (chip(y + d, x), u, layer)

    def piece(panel, q, along, across):
        return panel.at[pl.ds(tile_of(q, along, across) * 16 + q * 4, 4)]

    def panel_send(which, q, phase, step, j):
        panel = (pan, span)[which]
        at = step if phase == 0 else 3 + step * 4 + j
        part_of = piece(panel, q, step, 0) if phase == 0 else piece(panel, q, j, step)
        send(part_of, part_of, pan_send.at[which, q, at], pan_recv.at[which, q, at], target(q, phase))

    def panel_arrived(which, q, phase, step, j):
        panel = (pan, span)[which]
        at = step if phase == 0 else 3 + step * 4 + j
        part_of = piece(panel, q, step + 1, 0) if phase == 0 else piece(panel, q, j, step + 1)
        arrived(part_of, pan_send.at[which, q, at], pan_recv.at[which, q, at], target(q, phase))

    def panel_begin(which):
        for q in range(4):
            panel_send(which, q, 0, 0, 0)
        for q in range(4):
            panel_send(which, q, 1, 0, 0)

    def panel_round(which, n):
        for q in range(4):
            if n < 3:
                panel_arrived(which, q, 0, n, 0)
                if n < 2:
                    panel_send(which, q, 0, n + 1, 0)
                panel_send(which, q, 1, 0, n + 1)
            else:
                step, j = (n - 3) // 4, (n - 3) % 4
                panel_arrived(which, q, 1, step, j)
                if step < 2:
                    panel_send(which, q, 1, step + 1, j)

    def z_piece(array, width, pieces, e, step):
        d = 1 - 2 * (e % 2)
        size = width // pieces
        return array.at[pl.ds(((u - d * step) % NZ) * width + e * size, size)]

    def z_send(array, width, pieces, sems, e, step):
        d = 1 - 2 * (e % 2)
        part_of = z_piece(array, width, pieces, e, step)
        send(part_of, part_of, sems[0].at[e, step], sems[1].at[e, step], (r, (u + d) % NZ, layer))

    def z_round(array, width, pieces, sems, n):
        for e in range(pieces):
            d = 1 - 2 * (e % 2)
            part_of = z_piece(array, width, pieces, e, n + 1)
            arrived(part_of, sems[0].at[e, n], sems[1].at[e, n], (r, (u + d) % NZ, layer))
            if n + 1 < NZ - 1:
                z_send(array, width, pieces, sems, e, n + 1)

    own[0].wait()
    for q in range(4):
        panel_send(0, q, 0, 0, 0)
    own[1].wait()
    f1_sems, p1_sems = (f1_send, f1_recv), (p1_send, p1_recv)
    for e in range(2):
        z_send(f1_all, 8, 2, f1_sems, e, 0)
    for q in range(4):
        panel_send(0, q, 1, 0, 0)
    own[2].wait()

    for step in range(1, TILES):
        arrived(meta_row.at[(r - step) % TILES], meta_send.at[step], meta_recv.at[step], ((r + step) % TILES, u, layer))
    for step in range(1, NZ):
        at = TILES + step
        arrived(meta_z.at[(u - step) % NZ], meta_send.at[at], meta_recv.at[at], (r, (u + step) % NZ, layer))
    arrived(meta_core.at[other], meta_send.at[0], meta_recv.at[0], (r, u, other))
    tables = [
        pltpu.make_async_copy(meta_row, row_s, smem_sem.at[0]),
        pltpu.make_async_copy(meta_z, z_s, smem_sem.at[1]),
        pltpu.make_async_copy(meta_core, core_s, smem_sem.at[2]),
    ]
    for copy in tables:
        copy.start()

    for n in range(15):
        if n == 11:
            panel_begin(1)
        panel_round(0, n)
        if n < NZ - 1:
            z_round(f1_all, 8, 2, f1_sems, n)
    for copy in tables:
        copy.wait()

    def choose(panel, index):
        return panel[index]

    def first_row(i, carry):
        for c in range(NZ):
            k = z_s[c, i, F1C]
            t = lax.shift_right_logical(k, 4)
            base = t * 16 + c * 2
            n0, n1 = row_s[t, c, P0C], row_s[t, c, P0C + 1]
            for o in range(4):
                want = core_s[o // 2, i, P1F + o % 2]
                index = jnp.where(n0 == want, base, jnp.where(n1 == want, base + 1, ZERO))
                rhs[c * B:(c + 1) * B, o * B:(o + 1) * B] = choose(pan, index)
        lhs = jnp.concatenate([f1_all[c * 8 + i] for c in range(NZ)], axis=1)
        total = jnp.dot(lhs, rhs[...], preferred_element_type=jnp.float32)
        part[0, i] = total[:, :2 * B]
        part[1, i] = total[:, 2 * B:]
        return carry

    def part_send_row(i):
        send(part.at[other, i], part_in.at[i], part_send.at[i], part_recv.at[i], (r, u, other))

    for h in range(4):
        lax.fori_loop(2 * h, 2 * h + 2, first_row, 0)
        part_send_row(2 * h)
        part_send_row(2 * h + 1)
        if h < 3:
            panel_round(1, h)

    def finish_row(i, carry):
        total = (part[layer, i] + part_in[i]).astype(jnp.bfloat16)
        for o in range(2):
            block = total[:, o * B:(o + 1) * B]
            p1_all[u * 16 + i * 2 + o] = block
            p1_ref[i, o] = block
        return carry

    for e in range(4):
        for i in (2 * e, 2 * e + 1):
            arrived(part_in.at[i], part_send.at[i], part_recv.at[i], (r, u, other))
        lax.fori_loop(2 * e, 2 * e + 2, finish_row, 0)
        z_send(p1_all, 16, 4, p1_sems, e, 0)

    for n in range(12):
        panel_round(1, n + 3)
        if n < NZ - 1:
            z_round(p1_all, 16, 4, p1_sems, n)

    def second_row(i, carry):
        for c in range(NZ):
            for a in range(2):
                k = z_s[c, i, P1F + a]
                t = lax.shift_right_logical(k, 4)
                base = t * 16 + c * 2
                n0, n1 = row_s[t, c, SC], row_s[t, c, SC + 1]
                at = c * 2 + a
                for o in range(2):
                    want = core_s[o, i, QF]
                    index = jnp.where(n0 == want, base, jnp.where(n1 == want, base + 1, ZERO))
                    rhs_q[at * B:(at + 1) * B, o * B:(o + 1) * B] = choose(span, index)
        lhs = jnp.concatenate([p1_all[c * 16 + i * 2 + a] for c in range(NZ) for a in range(2)], axis=1)
        total = jnp.dot(lhs, rhs_q[...], preferred_element_type=jnp.float32)
        q_part[0, i] = total[:, :B].astype(jnp.bfloat16)
        q_part[1, i] = total[:, B:].astype(jnp.bfloat16)
        return carry

    for h in range(2):
        lax.fori_loop(4 * h, 4 * h + 4, second_row, 0)
        rows = pl.ds(4 * h, 4)
        send(q_part.at[other, rows], q_in.at[rows], q_send.at[h], q_recv.at[h], (r, u, other))
    for h in range(2):
        rows = pl.ds(4 * h, 4)
        arrived(q_in.at[rows], q_send.at[h], q_recv.at[h], (r, u, other))
        both = q_part[layer, rows].astype(jnp.float32) + q_in[rows].astype(jnp.float32)
        q_ref[rows] = both.astype(jnp.bfloat16)
    for copy in sent:
        copy.wait_send()


def dense(f1_vals, f1_cols, p0_vals, p0_cols, s_vals, s_cols, p1_filter, q_filter):
    meta = jnp.concatenate([f1_cols, p0_cols, s_cols, p1_filter, q_filter], axis=1)
    meta = jnp.pad(meta, ((0, 0), (0, B - meta.shape[1])))
    bf16, f32, i32 = jnp.bfloat16, jnp.float32, jnp.int32
    dma = pltpu.SemaphoreType.DMA
    p1, q = pl.pallas_call(
        dense_kernel,
        out_shape=(
            jax.ShapeDtypeStruct((ROWS, 2, B, B), bf16),
            jax.ShapeDtypeStruct((ROWS, B, B), bf16),
        ),
        in_specs=[pl.BlockSpec(memory_space=pltpu.VMEM)] + [pl.BlockSpec(memory_space=pl.ANY)] * 3,
        out_specs=(pl.BlockSpec(memory_space=pltpu.VMEM),) * 2,
        scratch_shapes=[
            pltpu.VMEM((TILES * 16 + 1, B, B), bf16),
            pltpu.VMEM((TILES * 16 + 1, B, B), bf16),
            pltpu.VMEM((NZ * 8, B, B), bf16),
            pltpu.VMEM((NZ * 16, B, B), bf16),
            pltpu.VMEM((NZ * B, 4 * B), bf16),
            pltpu.VMEM((NZ * 2 * B, 2 * B), bf16),
            pltpu.VMEM((2, ROWS, B, 2 * B), f32),
            pltpu.VMEM((ROWS, B, 2 * B), f32),
            pltpu.VMEM((2, ROWS, B, B), bf16),
            pltpu.VMEM((ROWS, B, B), bf16),
            pltpu.VMEM((TILES, 8, B), i32),
            pltpu.VMEM((NZ, 8, B), i32),
            pltpu.VMEM((2, 8, B), i32),
            pltpu.SMEM((TILES, 8, B), i32),
            pltpu.SMEM((NZ, 8, B), i32),
            pltpu.SMEM((2, 8, B), i32),
            dma((3,)),
            dma((TILES + NZ,)), dma((TILES + NZ,)),
            dma((2, 4, 15)), dma((2, 4, 15)),
            dma((2, NZ - 1)), dma((2, NZ - 1)),
            dma((ROWS,)), dma((ROWS,)),
            dma((4, NZ - 1)), dma((4, NZ - 1)),
            dma((2,)), dma((2,)),
            dma((3,)),
        ],
        compiler_params=pltpu.CompilerParams(
            collective_id=1, has_side_effects=True, vmem_limit_bytes=56 * 1024 * 1024
        ),
    )(
        meta,
        f1_vals.reshape(ROWS, B, B),
        p0_vals.reshape(16, B, B),
        s_vals.reshape(16, B, B),
    )
    return p1, q.reshape(ROWS, 1, B, B)


def body(*args):
    p1, q, flag = fast(*args)
    return lax.cond(
        flag[0, 0] > 0,
        lambda p1, q, *args: dense(*args),
        lambda p1, q, *args: (p1, q),
        p1, q.reshape(ROWS, 1, B, B), *args,
    )


def solution(mesh):
    return jax.shard_map(
        body,
        mesh=mesh,
        in_specs=(
            P("row", ("col", "layer"), None, None),
            P("row", ("col", "layer")),
            P(("row", "layer"), "col", None, None),
            P(("row", "layer"), "col"),
            P(("row", "layer"), "col", None, None),
            P(("row", "layer"), "col"),
            P("row", ("col", "layer")),
            P("row", ("col", "layer")),
        ),
        out_specs=(P("row", ("col", "layer"), None, None), P("row", ("col", "layer"), None, None)),
        check_vma=False,
    )
```

```python
import jax
import jax.numpy as jnp
from jax import lax
from jax.experimental import pallas as pl
from jax.experimental.pallas import tpu as pltpu
from jax.sharding import PartitionSpec as P

MESH = pl.DeviceIdType.MESH
B = 128
SIDE = 4
NZ = 8
ROWS = 8
TILES = SIDE * SIDE
CAP = 11
HALF = 6
PACKED = 65
BLOCKS = PACKED + 6 * CAP
F32, I32, BF16 = jnp.float32, jnp.int32, jnp.bfloat16


def inside(index, count):
    return lax.max(lax.min(index, count - 1), 0)


def fast_kernel(
    f1c_ref, p0c_ref, sc_ref, p1f_ref, qf_ref, f1_ref, p0_ref, s_ref, p1_ref, q_ref, flag_ref,
    whole_p, whole_s, buf_p, buf_s, outs, relays, f1_all, p1_all, rhs, rhs_q, part, part_in, q_part, q_in,
    own_tile, row_tiles, z_tiles, core_tiles, demand, code, code_in, index_v, list_v, index_s, list_s,
    flag_own, flag_row, flag_z, flag_core,
    local_sem, meta_send, meta_recv, code_send, code_recv, pan_send, pan_recv, pack_send, pack_recv,
    rel_send, rel_recv, f1_send, f1_recv, part_send, part_recv, p1_send, p1_recv, q_send, q_recv,
    flag_send, flag_recv, smem_sem,
):
    r = lax.axis_index("row")
    u = lax.axis_index("col")
    layer = lax.axis_index("layer")
    x, y = r % SIDE, r // SIDE
    other = 1 - layer
    whole, bufs = (whole_p, whole_s), (buf_p, buf_s)

    def chip(y_at, x_at):
        return ((y_at % SIDE) * SIDE + x_at % SIDE, u, layer)

    own = []
    for which, ref in ((0, p0_ref), (1, s_ref)):
        own.append(pltpu.make_async_copy(ref.at[pl.ds(0, 8)], whole[which].at[pl.ds(1 + x * 8, 8)], local_sem.at[2 * which]))
        own.append(pltpu.make_async_copy(ref.at[pl.ds(8, 8)], whole[which].at[pl.ds(33 + y * 8, 8)], local_sem.at[2 * which + 1]))
    own.append(pltpu.make_async_copy(f1_ref, f1_all.at[pl.ds(u * 8, 8)], local_sem.at[4]))
    for copy in own:
        copy.start()

    barrier = pltpu.get_barrier_semaphore()
    for step in range(1, TILES):
        pl.semaphore_signal(barrier, inc=1, device_id=((r + step) % TILES, u, layer), device_id_type=MESH)
    for step in range(1, NZ):
        pl.semaphore_signal(barrier, inc=1, device_id=(r, (u + step) % NZ, layer), device_id_type=MESH)
    pl.semaphore_signal(barrier, inc=1, device_id=(r, u, other), device_id_type=MESH)

    for panel in whole:
        panel[0] = jnp.zeros((B, B), BF16)
    sub8 = lax.broadcasted_iota(I32, (8, B), 0)
    lane8 = lax.broadcasted_iota(I32, (8, B), 1)

    own_tile[...] = jnp.full((8, B), -1, I32)
    for at, ref in ((0, p0c_ref), (2, sc_ref), (4, f1c_ref), (5, p1f_ref), (7, qf_ref)):
        own_tile[at:at + ref.shape[0], 0:8] = ref[...]
    row_tiles[r] = own_tile[...]
    z_tiles[u] = own_tile[...]
    core_tiles[layer] = own_tile[...]
    pl.semaphore_wait(barrier, TILES - 1 + NZ - 1 + 1)

    sent = []

    def remote(src, dst, send_sem, recv_sem, device):
        return pltpu.make_async_remote_copy(
            src_ref=src, dst_ref=dst, send_sem=send_sem, recv_sem=recv_sem,
            device_id=device, device_id_type=MESH,
        )

    def send(src, dst, send_sem, recv_sem, device):
        copy = remote(src, dst, send_sem, recv_sem, device)
        copy.start()
        sent.append(copy)

    def arrived(dst, send_sem, recv_sem, device):
        remote(dst, dst, send_sem, recv_sem, device).wait_recv()

    def row_peer(step):
        return ((r + step) % TILES, u, layer)

    def z_peer(step):
        return (r, (u + step) % NZ, layer)

    core_peer = (r, u, other)

    for step in range(1, NZ):
        at = TILES + step
        send(own_tile, z_tiles.at[u], meta_send.at[at], meta_recv.at[at], z_peer(step))
    send(own_tile, core_tiles.at[layer], meta_send.at[0], meta_recv.at[0], core_peer)
    for step in range(1, TILES):
        send(own_tile, row_tiles.at[r], meta_send.at[step], meta_recv.at[step], row_peer(step))

    def along(axis, d):
        return chip(y, x + d) if axis == 0 else chip(y + d, x)

    def quarter(which, h, q, d):
        at = (x if h == 0 else y) - d
        return whole[which].at[pl.ds(1 + 32 * h + (at % SIDE) * 8 + q * 4, 4)]

    def panel_begin(which):
        for n in range(2):
            for h in range(2):
                for way in (0, 1):
                    q, d = n if way == 0 else 1 - n, 1 - 2 * way
                    part_of = quarter(which, h, q, 0)
                    send(part_of, part_of, pan_send.at[which, h, way, n], pan_recv.at[which, h, way, n], along(h, d))

    def panel_round(which, n):
        for h in range(2):
            for way in (0, 1):
                d = 1 - 2 * way
                q = (n if way == 0 else 1 - n) if n < 2 else way
                part_of = quarter(which, h, q, d if n < 2 else 2 * d)
                arrived(part_of, pan_send.at[which, h, way, n], pan_recv.at[which, h, way, n], along(h, d))
                if n == 0:
                    send(part_of, part_of, pan_send.at[which, h, way, 2], pan_recv.at[which, h, way, 2], along(h, d))

    def packet(which, h, d):
        return bufs[which].at[pl.ds(PACKED + (h * 3 + d - 1) * CAP, CAP)]

    def half_of(ref, e):
        return ref.at[pl.ds(e * HALF, HALF if e == 0 else CAP - HALF)]

    def relayed(which, h, e):
        return relays.at[which, h, e, pl.ds(0, HALF if e == 0 else CAP - HALF)]

    def relay(which):
        for h in range(2):
            for e, way in ((0, 1), (1, -1)):
                arrived(relayed(which, h, e), rel_send.at[which, h, e], rel_recv.at[which, h, e], along(1 - h, way))
                send(
                    relayed(which, h, e), half_of(packet(which, h, 2), e),
                    pack_send.at[which, h, 3 + e], pack_recv.at[which, h, 3 + e], along(1 - h, way),
                )

    def packets_arrived(which):
        for h in range(2):
            for d in (1, 3):
                arrived(packet(which, h, d), pack_send.at[which, h, d - 1], pack_recv.at[which, h, d - 1], along(1 - h, 1))
            for e in range(2):
                arrived(half_of(packet(which, h, 2), e), pack_send.at[which, h, 3 + e], pack_recv.at[which, h, 3 + e], along(1 - h, 1))

    def z_piece(array, width, pieces, e, step):
        d = 1 - 2 * (e % 2)
        size = width // pieces
        return array.at[pl.ds(((u - d * step) % NZ) * width + e * size, size)]

    def z_send(array, width, pieces, sems, e, step):
        d = 1 - 2 * (e % 2)
        part_of = z_piece(array, width, pieces, e, step)
        send(part_of, part_of, sems[0].at[e, step], sems[1].at[e, step], z_peer(d))

    def z_round(array, width, pieces, sems, n, only=None):
        for e in range(pieces) if only is None else only:
            d = 1 - 2 * (e % 2)
            arrived(z_piece(array, width, pieces, e, n + 1), sems[0].at[e, n], sems[1].at[e, n], z_peer(d))
            if n + 1 < NZ - 1:
                z_send(array, width, pieces, sems, e, n + 1)

    f1_sems, p1_sems = (f1_send, f1_recv), (p1_send, p1_recv)
    own[0].wait()
    own[1].wait()
    panel_begin(0)
    own[4].wait()
    for e in range(4):
        z_send(f1_all, 8, 4, f1_sems, e, 0)
    own[2].wait()
    own[3].wait()

    for step in range(1, NZ):
        at = TILES + step
        arrived(z_tiles.at[(u - step) % NZ], meta_send.at[at], meta_recv.at[at], z_peer(step))
    arrived(core_tiles.at[other], meta_send.at[0], meta_recv.at[0], core_peer)

    def column_of(line):
        spread = jnp.where(sub8 == lane8, jnp.broadcast_to(line.astype(F32), (8, B)), 0.0)
        return jnp.broadcast_to(jnp.sum(spread, axis=1, keepdims=True), (8, B))

    for at in range(3):
        merged = jnp.zeros((8, B), F32)
        for c in range(NZ):
            merged = jnp.where(lane8 == c, column_of(z_tiles[c, 4 + at:5 + at, :]), merged)
        demand[at] = merged.astype(I32)
    for o in range(4):
        demand[3 + o] = column_of(core_tiles[o // 2, 5 + o % 2:6 + o % 2, :]).astype(I32)
    for o in range(2):
        demand[7 + o] = column_of(core_tiles[o, 7:8, :]).astype(I32)

    for step in range(1, TILES):
        arrived(row_tiles.at[(r - step) % TILES], meta_send.at[step], meta_recv.at[step], row_peer(step))

    tile = lax.broadcasted_iota(I32, (TILES, B), 0)
    lane = lax.broadcasted_iota(I32, (TILES, B), 1)
    tile_y, tile_x = lax.shift_right_logical(tile, 2), tile & 3
    upper = lane >= 4
    lane_a = lax.broadcasted_iota(I32, (B, B), 0)
    lane_b = lax.broadcasted_iota(I32, (B, B), 1)
    same = lax.shift_right_logical(lane_a, 2) == lax.shift_right_logical(lane_b, 2)
    one, nil = jnp.ones((), F32), jnp.zeros((), F32)
    lanes_all = jnp.where(same, one, nil)
    lanes_before = jnp.where(same & (lane_a < lane_b), one, nil)
    tile_a = lax.broadcasted_iota(I32, (TILES, TILES), 0)
    tile_b = lax.broadcasted_iota(I32, (TILES, TILES), 1)
    before = tile_b < tile_a
    same_y = lax.shift_right_logical(tile_a, 2) == lax.shift_right_logical(tile_b, 2)
    same_x = (tile_a & 3) == (tile_b & 3)
    tiles_y = jnp.where(before & same_y, one, nil)
    tiles_x = jnp.where(before & same_x, one, nil)

    def dot(a, b):
        return jnp.dot(a, b, preferred_element_type=F32)

    name = [[row_tiles[:, 2 * which + w, :] for w in range(2)] for which in range(2)]

    def wide(at, i):
        return jnp.broadcast_to(demand[at, i:i + 1, :], (TILES, B))

    def matches(which):
        result = []
        for i in range(ROWS):
            wants = [wide(at, i) for at in (range(3, 7) if which == 0 else range(7, 9))]
            for at in (range(1) if which == 0 else range(1, 3)):
                hit = lax.shift_right_logical(wide(at, i), 4) == tile
                result.append([[hit & (name[which][w] == want) for w in range(2)] for want in wants])
        return result

    def needs(masks):
        total = []
        for w in range(2):
            need = masks[0][0][w]
            for row in masks:
                for slot in row:
                    need = need | slot[w]
            total.append(jnp.where(need, one, nil))
        return total

    def ranks(need):
        both = need[0] + need[1]
        all_of = dot(both, lanes_all)
        first = jnp.where(upper, dot(tiles_x, all_of), dot(tiles_y, all_of)) + dot(both, lanes_before)
        return [first, first + need[0]]

    within = (lane & 3) * 2
    place = 1 + jnp.where(upper, 32 + tile_y * 8 + within, tile_x * 8 + within)
    offset = jnp.where(upper, tile_x - x, tile_y - y) & 3
    here = offset == 0
    packed = PACKED + jnp.where(upper, 3 * CAP, 0) + (offset - 1) * CAP
    place_f, packed_f = place.astype(F32), packed.astype(F32)

    def own_code(which):
        masks = matches(which)
        need = needs(masks)
        rank = ranks(need)
        code[which] = (jnp.where(need[0] > 0.5, rank[0] + 1.0, 0.0) + 64.0 * jnp.where(need[1] > 0.5, rank[1] + 1.0, 0.0)).astype(I32)
        for axis in range(2):
            for d in (1, 2, 3):
                at = axis * 3 + d - 1
                send(
                    code.at[which], code_in.at[which, axis, 3 - d],
                    code_send.at[which, at], code_recv.at[which, axis * 3 + 3 - d], along(axis, d),
                )
        return masks, need, rank

    def own_index(which, masks, need, rank):
        spot, worst = [], jnp.zeros((TILES, B), F32)
        for w in range(2):
            fits = rank[w] < float(CAP)
            spot.append(jnp.where(here, place_f + float(w), jnp.where(fits, packed_f + rank[w], 0.0)))
            worst = worst + jnp.where((need[w] > 0.5) & jnp.logical_not(fits | here), one, nil)
        at = 0
        for row in masks:
            for slot in row:
                chosen = jnp.where(slot[0], spot[0], jnp.where(slot[1], spot[1], 0.0))
                line = jnp.sum(chosen, axis=0, keepdims=True)
                index_v[which, at:at + 1, :] = line.astype(I32)
                at += 1
        return worst

    def peer_lists(which):
        table = jnp.zeros((TILES, B), F32)
        for h in range(2):
            axis = 1 - h
            mine = (jnp.logical_not(upper) & (tile_y == y)) if h == 0 else (upper & (lane < 8) & (tile_x == x))
            for d in (1, 2, 3):
                at = axis * 3 + d - 1
                arrived(code_in.at[which, axis, d - 1], code_send.at[which, at], code_recv.at[which, at], along(axis, d))
                there = jnp.where(mine, code_in[which, axis, d - 1], 0)
                rank = [there & 63, lax.shift_right_logical(there, 6)]
                slots = jnp.zeros((TILES, B), F32)
                for j in range(CAP):
                    chosen = jnp.where(rank[0] == j + 1, place_f, 0.0) + jnp.where(rank[1] == j + 1, place_f + 1.0, 0.0)
                    line = jnp.sum(chosen, axis=0, keepdims=True)
                    slots = jnp.where(tile == j, jnp.broadcast_to(line, (TILES, B)), slots)
                column = jnp.broadcast_to(jnp.sum(slots, axis=1, keepdims=True), (TILES, B))
                table = jnp.where(lane == (which * 2 + h) * 3 + d - 1, column, table)
        return table

    found = own_code(0)
    panel_round(0, 0)
    z_round(f1_all, 8, 4, f1_sems, 0)
    lists = [pltpu.make_async_copy(list_v.at[w], list_s.at[w], smem_sem.at[w]) for w in range(2)]
    list_v[0] = peer_lists(0).astype(I32)
    lists[0].start()
    z_round(f1_all, 8, 4, f1_sems, 1)
    panel_round(0, 1)
    panel_round(0, 2)
    settle = [pltpu.make_async_copy(whole[w], bufs[w].at[pl.ds(0, PACKED)], local_sem.at[5 + w]) for w in range(2)]
    lists[0].wait()

    def pack(which, ref):
        for h in range(2):
            for d in (2, 1, 3):
                column = (which * 2 + h) * 3 + d - 1
                for j in range(CAP):
                    outs[which, h, d - 1, j] = whole[which][inside(ref[j, column], PACKED)]
                axis = 1 - h
                if d == 2:
                    for e, way in ((0, 1), (1, -1)):
                        send(
                            half_of(outs.at[which, h, 1], e), relayed(which, h, e),
                            rel_send.at[which, h, e], rel_recv.at[which, h, e], along(axis, way),
                        )
                else:
                    way = 1 if d == 1 else -1
                    send(
                        outs.at[which, h, d - 1], packet(which, h, 4 - d),
                        pack_send.at[which, h, d - 1], pack_recv.at[which, h, 3 - d], along(axis, way),
                    )

    pack(0, list_s.at[0])
    settle[0].start()
    z_round(f1_all, 8, 4, f1_sems, 2)
    found_s = own_code(1)
    z_round(f1_all, 8, 4, f1_sems, 3)
    over = own_index(0, *found)
    first_index = pltpu.make_async_copy(index_v.at[0], index_s.at[0], smem_sem.at[2])
    first_index.start()
    z_round(f1_all, 8, 4, f1_sems, 4)
    relay(0)
    panel_begin(1)
    z_round(f1_all, 8, 4, f1_sems, 5)
    list_v[1] = peer_lists(1).astype(I32)
    lists[1].start()
    over = over + own_index(1, *found_s)
    second_index = pltpu.make_async_copy(index_v.at[1], index_s.at[1], smem_sem.at[3])
    second_index.start()
    flag_own[0] = over[:8] + over[8:]
    z_round(f1_all, 8, 4, f1_sems, 6)
    first_index.wait()
    settle[0].wait()
    packets_arrived(0)
    lists[1].wait()

    def first_row(i, carry):
        for c in range(NZ):
            for o in range(4):
                rhs[c * B:(c + 1) * B, o * B:(o + 1) * B] = buf_p[inside(index_s[0, i * 4 + o, c], BLOCKS)]
        lhs = jnp.concatenate([f1_all[c * 8 + i] for c in range(NZ)], axis=1)
        total = dot(lhs, rhs[...])
        part[0, i] = total[:, :2 * B]
        part[1, i] = total[:, 2 * B:]
        return carry

    def part_send_row(i):
        send(part.at[other, i], part_in.at[i], part_send.at[i], part_recv.at[i], core_peer)

    def finish_row(i, carry):
        total = (part[layer, i] + part_in[i]).astype(BF16)
        for o in range(2):
            block = total[:, o * B:(o + 1) * B]
            p1_all[u * 16 + i * 2 + o] = block
            p1_ref[i, o] = block
        return carry

    def finish(e):
        for i in (2 * e, 2 * e + 1):
            arrived(part_in.at[i], part_send.at[i], part_recv.at[i], core_peer)
        lax.fori_loop(2 * e, 2 * e + 2, finish_row, 0)
        z_send(p1_all, 16, 4, p1_sems, e, 0)

    for h in range(4):
        lax.fori_loop(2 * h, 2 * h + 2, first_row, 0)
        part_send_row(2 * h)
        part_send_row(2 * h + 1)
        if h > 0:
            finish(h - 1)
        if h == 2:
            panel_round(1, 0)
    finish(3)

    for step in range(1, TILES):
        send(flag_own.at[0], flag_row.at[step - 1], flag_send.at[step - 1], flag_recv.at[step - 1], row_peer(step))
    z_round(p1_all, 16, 4, p1_sems, 0)
    panel_round(1, 1)
    panel_round(1, 2)
    pack(1, list_s.at[1])
    settle[1].start()
    z_round(p1_all, 16, 4, p1_sems, 1)
    total = flag_own[0]
    for step in range(1, TILES):
        arrived(flag_row.at[step - 1], flag_send.at[step - 1], flag_recv.at[step - 1], row_peer(step))
        total = total + flag_row[step - 1]
    flag_own[1] = total
    for step in range(1, NZ):
        at = TILES - 2 + step
        send(flag_own.at[1], flag_z.at[step - 1], flag_send.at[at], flag_recv.at[at], z_peer(step))
    z_round(p1_all, 16, 4, p1_sems, 2)
    relay(1)
    z_round(p1_all, 16, 4, p1_sems, 3)
    for step in range(1, NZ):
        at = TILES - 2 + step
        arrived(flag_z.at[step - 1], flag_send.at[at], flag_recv.at[at], z_peer(step))
        total = total + flag_z[step - 1]
    flag_own[2] = total
    at = TILES + NZ - 2
    send(flag_own.at[2], flag_core, flag_send.at[at], flag_recv.at[at], core_peer)
    z_round(p1_all, 16, 4, p1_sems, 4)
    arrived(flag_core, flag_send.at[at], flag_recv.at[at], core_peer)
    total = total + flag_core[...]
    flag_ref[0, 0] = jnp.where(jnp.sum(total) > 0.5, 1, 0)
    z_round(p1_all, 16, 4, p1_sems, 5)
    packets_arrived(1)
    settle[1].wait()
    second_index.wait()

    def second_row(i, carry):
        for c in range(NZ):
            for a in range(2):
                at = c * 2 + a
                for o in range(2):
                    rhs_q[at * B:(at + 1) * B, o * B:(o + 1) * B] = buf_s[inside(index_s[1, i * 4 + a * 2 + o, c], BLOCKS)]
        lhs = jnp.concatenate([p1_all[c * 16 + i * 2 + a] for c in range(NZ) for a in range(2)], axis=1)
        total = dot(lhs, rhs_q[...])
        q_part[0, i] = total[:, :B].astype(BF16)
        q_part[1, i] = total[:, B:].astype(BF16)
        return carry

    for h in range(4):
        z_round(p1_all, 16, 4, p1_sems, NZ - 2, (h,))
        lax.fori_loop(2 * h, 2 * h + 2, second_row, 0)
        rows = pl.ds(2 * h, 2)
        send(q_part.at[other, rows], q_in.at[rows], q_send.at[h], q_recv.at[h], core_peer)
    for h in range(4):
        rows = pl.ds(2 * h, 2)
        arrived(q_in.at[rows], q_send.at[h], q_recv.at[h], core_peer)
        both = q_part[layer, rows].astype(F32) + q_in[rows].astype(F32)
        q_ref[rows] = both.astype(BF16)
    for copy in sent:
        copy.wait_send()


def fast(f1_vals, f1_cols, p0_vals, p0_cols, s_vals, s_cols, p1_filter, q_filter):
    dma = pltpu.SemaphoreType.DMA
    vmem = pl.BlockSpec(memory_space=pltpu.VMEM)
    return pl.pallas_call(
        fast_kernel,
        out_shape=(
            jax.ShapeDtypeStruct((ROWS, 2, B, B), BF16),
            jax.ShapeDtypeStruct((ROWS, B, B), BF16),
            jax.ShapeDtypeStruct((1, 1), I32),
        ),
        in_specs=[vmem] * 5 + [pl.BlockSpec(memory_space=pl.ANY)] * 3,
        out_specs=(vmem, vmem, pl.BlockSpec(memory_space=pltpu.SMEM)),
        scratch_shapes=[
            pltpu.VMEM((PACKED, B, B), BF16),
            pltpu.VMEM((PACKED, B, B), BF16),
            pltpu.VMEM((BLOCKS, B, B), BF16),
            pltpu.VMEM((BLOCKS, B, B), BF16),
            pltpu.VMEM((2, 2, 3, CAP, B, B), BF16),
            pltpu.VMEM((2, 2, 2, HALF, B, B), BF16),
            pltpu.VMEM((NZ * 8, B, B), BF16),
            pltpu.VMEM((NZ * 16, B, B), BF16),
            pltpu.VMEM((NZ * B, 4 * B), BF16),
            pltpu.VMEM((NZ * 2 * B, 2 * B), BF16),
            pltpu.VMEM((2, ROWS, B, 2 * B), F32),
            pltpu.VMEM((ROWS, B, 2 * B), F32),
            pltpu.VMEM((2, ROWS, B, B), BF16),
            pltpu.VMEM((ROWS, B, B), BF16),
            pltpu.VMEM((8, B), I32),
            pltpu.VMEM((TILES, 8, B), I32),
            pltpu.VMEM((NZ, 8, B), I32),
            pltpu.VMEM((2, 8, B), I32),
            pltpu.VMEM((9, 8, B), I32),
            pltpu.VMEM((2, TILES, B), I32),
            pltpu.VMEM((2, 2, 3, TILES, B), I32),
            pltpu.VMEM((2, 32, B), I32),
            pltpu.VMEM((2, TILES, B), I32),
            pltpu.SMEM((2, 32, B), I32),
            pltpu.SMEM((2, TILES, B), I32),
            pltpu.VMEM((3, 8, B), F32),
            pltpu.VMEM((TILES - 1, 8, B), F32),
            pltpu.VMEM((NZ - 1, 8, B), F32),
            pltpu.VMEM((8, B), F32),
            dma((7,)),
            dma((TILES + NZ,)), dma((TILES + NZ,)),
            dma((2, 6)), dma((2, 6)),
            dma((2, 2, 2, 3)), dma((2, 2, 2, 3)),
            dma((2, 2, 5)), dma((2, 2, 5)),
            dma((2, 2, 2)), dma((2, 2, 2)),
            dma((4, NZ - 1)), dma((4, NZ - 1)),
            dma((ROWS,)), dma((ROWS,)),
            dma((4, NZ - 1)), dma((4, NZ - 1)),
            dma((4,)), dma((4,)),
            dma((TILES + NZ - 1,)), dma((TILES + NZ - 1,)),
            dma((4,)),
        ],
        compiler_params=pltpu.CompilerParams(
            collective_id=0, has_side_effects=True, vmem_limit_bytes=56 * 1024 * 1024
        ),
    )(
        f1_cols.T, p0_cols.T, s_cols.T, p1_filter.T, q_filter.T,
        f1_vals.reshape(ROWS, B, B),
        p0_vals.reshape(16, B, B),
        s_vals.reshape(16, B, B),
    )


ZERO = TILES * 16
F1C, P0C, SC, P1F, QF = 0, 1, 3, 5, 7


def dense_kernel(
    meta_ref, f1_ref, p0_ref, s_ref, p1_ref, q_ref,
    pan, span, f1_all, p1_all, rhs, rhs_q, part, part_in, q_part, q_in,
    meta_row, meta_z, meta_core, row_s, z_s, core_s,
    local_sem, meta_send, meta_recv, pan_send, pan_recv, f1_send, f1_recv,
    part_send, part_recv, p1_send, p1_recv, q_send, q_recv, smem_sem,
):
    r = lax.axis_index("row")
    u = lax.axis_index("col")
    layer = lax.axis_index("layer")
    x, y = r % SIDE, r // SIDE
    other = 1 - layer

    def chip(y_at, x_at):
        return (y_at % SIDE) * SIDE + x_at % SIDE

    own = [
        pltpu.make_async_copy(p0_ref, pan.at[pl.ds(r * 16, 16)], local_sem.at[0]),
        pltpu.make_async_copy(f1_ref, f1_all.at[pl.ds(u * 8, 8)], local_sem.at[1]),
        pltpu.make_async_copy(s_ref, span.at[pl.ds(r * 16, 16)], local_sem.at[2]),
    ]
    for copy in own:
        copy.start()

    barrier = pltpu.get_barrier_semaphore()
    for step in range(1, TILES):
        pl.semaphore_signal(barrier, inc=1, device_id=((r + step) % TILES, u, layer), device_id_type=MESH)
    for step in range(1, NZ):
        pl.semaphore_signal(barrier, inc=1, device_id=(r, (u + step) % NZ, layer), device_id_type=MESH)
    pl.semaphore_signal(barrier, inc=1, device_id=(r, u, other), device_id_type=MESH)

    pan[ZERO] = jnp.zeros((B, B), jnp.bfloat16)
    span[ZERO] = jnp.zeros((B, B), jnp.bfloat16)
    meta_row[r] = meta_ref[...]
    meta_z[u] = meta_ref[...]
    meta_core[layer] = meta_ref[...]
    pl.semaphore_wait(barrier, TILES - 1 + NZ - 1 + 1)

    sent = []

    def send(src, dst, send_sem, recv_sem, device):
        copy = pltpu.make_async_remote_copy(
            src_ref=src, dst_ref=dst, send_sem=send_sem, recv_sem=recv_sem,
            device_id=device, device_id_type=MESH,
        )
        copy.start()
        sent.append(copy)

    def arrived(dst, send_sem, recv_sem, device):
        pltpu.make_async_remote_copy(
            src_ref=dst, dst_ref=dst, send_sem=send_sem, recv_sem=recv_sem,
            device_id=device, device_id_type=MESH,
        ).wait_recv()

    for step in range(1, TILES):
        send(meta_ref, meta_row.at[r], meta_send.at[step], meta_recv.at[step], ((r + step) % TILES, u, layer))
    for step in range(1, NZ):
        at = TILES + step
        send(meta_ref, meta_z.at[u], meta_send.at[at], meta_recv.at[at], (r, (u + step) % NZ, layer))
    send(meta_ref, meta_core.at[layer], meta_send.at[0], meta_recv.at[0], (r, u, other))

    ways = ((0, 1), (0, -1), (1, 1), (1, -1))

    def tile_of(q, along, across):
        first, d = ways[q]
        if first == 0:
            return chip(y - d * across, x - d * along)
        return chip(y - d * along, x - d * across)

    def target(q, phase):
        first, d = ways[q]
        if (first + phase) % 2 == 0:
            return (chip(y, x + d), u, layer)
        return (chip(y + d, x), u, layer)

    def piece(panel, q, along, across):
        return panel.at[pl.ds(tile_of(q, along, across) * 16 + q * 4, 4)]

    def panel_send(which, q, phase, step, j):
        panel = (pan, span)[which]
        at = step if phase == 0 else 3 + step * 4 + j
        part_of = piece(panel, q, step, 0) if phase == 0 else piece(panel, q, j, step)
        send(part_of, part_of, pan_send.at[which, q, at], pan_recv.at[which, q, at], target(q, phase))

    def panel_arrived(which, q, phase, step, j):
        panel = (pan, span)[which]
        at = step if phase == 0 else 3 + step * 4 + j
        part_of = piece(panel, q, step + 1, 0) if phase == 0 else piece(panel, q, j, step + 1)
        arrived(part_of, pan_send.at[which, q, at], pan_recv.at[which, q, at], target(q, phase))

    def panel_begin(which):
        for q in range(4):
            panel_send(which, q, 0, 0, 0)
        for q in range(4):
            panel_send(which, q, 1, 0, 0)

    def panel_round(which, n):
        for q in range(4):
            if n < 3:
                panel_arrived(which, q, 0, n, 0)
                if n < 2:
                    panel_send(which, q, 0, n + 1, 0)
                panel_send(which, q, 1, 0, n + 1)
            else:
                step, j = (n - 3) // 4, (n - 3) % 4
                panel_arrived(which, q, 1, step, j)
                if step < 2:
                    panel_send(which, q, 1, step + 1, j)

    def z_piece(array, width, pieces, e, step):
        d = 1 - 2 * (e % 2)
        size = width // pieces
        return array.at[pl.ds(((u - d * step) % NZ) * width + e * size, size)]

    def z_send(array, width, pieces, sems, e, step):
        d = 1 - 2 * (e % 2)
        part_of = z_piece(array, width, pieces, e, step)
        send(part_of, part_of, sems[0].at[e, step], sems[1].at[e, step], (r, (u + d) % NZ, layer))

    def z_round(array, width, pieces, sems, n):
        for e in range(pieces):
            d = 1 - 2 * (e % 2)
            part_of = z_piece(array, width, pieces, e, n + 1)
            arrived(part_of, sems[0].at[e, n], sems[1].at[e, n], (r, (u + d) % NZ, layer))
            if n + 1 < NZ - 1:
                z_send(array, width, pieces, sems, e, n + 1)

    own[0].wait()
    for q in range(4):
        panel_send(0, q, 0, 0, 0)
    own[1].wait()
    f1_sems, p1_sems = (f1_send, f1_recv), (p1_send, p1_recv)
    for e in range(2):
        z_send(f1_all, 8, 2, f1_sems, e, 0)
    for q in range(4):
        panel_send(0, q, 1, 0, 0)
    own[2].wait()

    for step in range(1, TILES):
        arrived(meta_row.at[(r - step) % TILES], meta_send.at[step], meta_recv.at[step], ((r + step) % TILES, u, layer))
    for step in range(1, NZ):
        at = TILES + step
        arrived(meta_z.at[(u - step) % NZ], meta_send.at[at], meta_recv.at[at], (r, (u + step) % NZ, layer))
    arrived(meta_core.at[other], meta_send.at[0], meta_recv.at[0], (r, u, other))
    tables = [
        pltpu.make_async_copy(meta_row, row_s, smem_sem.at[0]),
        pltpu.make_async_copy(meta_z, z_s, smem_sem.at[1]),
        pltpu.make_async_copy(meta_core, core_s, smem_sem.at[2]),
    ]
    for copy in tables:
        copy.start()

    for n in range(15):
        if n == 11:
            panel_begin(1)
        panel_round(0, n)
        if n < NZ - 1:
            z_round(f1_all, 8, 2, f1_sems, n)
    for copy in tables:
        copy.wait()

    def choose(panel, index):
        return panel[index]

    def first_row(i, carry):
        for c in range(NZ):
            k = z_s[c, i, F1C]
            t = lax.shift_right_logical(k, 4)
            base = t * 16 + c * 2
            n0, n1 = row_s[t, c, P0C], row_s[t, c, P0C + 1]
            for o in range(4):
                want = core_s[o // 2, i, P1F + o % 2]
                index = jnp.where(n0 == want, base, jnp.where(n1 == want, base + 1, ZERO))
                rhs[c * B:(c + 1) * B, o * B:(o + 1) * B] = choose(pan, index)
        lhs = jnp.concatenate([f1_all[c * 8 + i] for c in range(NZ)], axis=1)
        total = jnp.dot(lhs, rhs[...], preferred_element_type=jnp.float32)
        part[0, i] = total[:, :2 * B]
        part[1, i] = total[:, 2 * B:]
        return carry

    def part_send_row(i):
        send(part.at[other, i], part_in.at[i], part_send.at[i], part_recv.at[i], (r, u, other))

    for h in range(4):
        lax.fori_loop(2 * h, 2 * h + 2, first_row, 0)
        part_send_row(2 * h)
        part_send_row(2 * h + 1)
        if h < 3:
            panel_round(1, h)

    def finish_row(i, carry):
        total = (part[layer, i] + part_in[i]).astype(jnp.bfloat16)
        for o in range(2):
            block = total[:, o * B:(o + 1) * B]
            p1_all[u * 16 + i * 2 + o] = block
            p1_ref[i, o] = block
        return carry

    for e in range(4):
        for i in (2 * e, 2 * e + 1):
            arrived(part_in.at[i], part_send.at[i], part_recv.at[i], (r, u, other))
        lax.fori_loop(2 * e, 2 * e + 2, finish_row, 0)
        z_send(p1_all, 16, 4, p1_sems, e, 0)

    for n in range(12):
        panel_round(1, n + 3)
        if n < NZ - 1:
            z_round(p1_all, 16, 4, p1_sems, n)

    def second_row(i, carry):
        for c in range(NZ):
            for a in range(2):
                k = z_s[c, i, P1F + a]
                t = lax.shift_right_logical(k, 4)
                base = t * 16 + c * 2
                n0, n1 = row_s[t, c, SC], row_s[t, c, SC + 1]
                at = c * 2 + a
                for o in range(2):
                    want = core_s[o, i, QF]
                    index = jnp.where(n0 == want, base, jnp.where(n1 == want, base + 1, ZERO))
                    rhs_q[at * B:(at + 1) * B, o * B:(o + 1) * B] = choose(span, index)
        lhs = jnp.concatenate([p1_all[c * 16 + i * 2 + a] for c in range(NZ) for a in range(2)], axis=1)
        total = jnp.dot(lhs, rhs_q[...], preferred_element_type=jnp.float32)
        q_part[0, i] = total[:, :B].astype(jnp.bfloat16)
        q_part[1, i] = total[:, B:].astype(jnp.bfloat16)
        return carry

    for h in range(2):
        lax.fori_loop(4 * h, 4 * h + 4, second_row, 0)
        rows = pl.ds(4 * h, 4)
        send(q_part.at[other, rows], q_in.at[rows], q_send.at[h], q_recv.at[h], (r, u, other))
    for h in range(2):
        rows = pl.ds(4 * h, 4)
        arrived(q_in.at[rows], q_send.at[h], q_recv.at[h], (r, u, other))
        both = q_part[layer, rows].astype(jnp.float32) + q_in[rows].astype(jnp.float32)
        q_ref[rows] = both.astype(jnp.bfloat16)
    for copy in sent:
        copy.wait_send()


def dense(f1_vals, f1_cols, p0_vals, p0_cols, s_vals, s_cols, p1_filter, q_filter):
    meta = jnp.concatenate([f1_cols, p0_cols, s_cols, p1_filter, q_filter], axis=1)
    meta = jnp.pad(meta, ((0, 0), (0, B - meta.shape[1])))
    bf16, f32, i32 = jnp.bfloat16, jnp.float32, jnp.int32
    dma = pltpu.SemaphoreType.DMA
    p1, q = pl.pallas_call(
        dense_kernel,
        out_shape=(
            jax.ShapeDtypeStruct((ROWS, 2, B, B), bf16),
            jax.ShapeDtypeStruct((ROWS, B, B), bf16),
        ),
        in_specs=[pl.BlockSpec(memory_space=pltpu.VMEM)] + [pl.BlockSpec(memory_space=pl.ANY)] * 3,
        out_specs=(pl.BlockSpec(memory_space=pltpu.VMEM),) * 2,
        scratch_shapes=[
            pltpu.VMEM((TILES * 16 + 1, B, B), bf16),
            pltpu.VMEM((TILES * 16 + 1, B, B), bf16),
            pltpu.VMEM((NZ * 8, B, B), bf16),
            pltpu.VMEM((NZ * 16, B, B), bf16),
            pltpu.VMEM((NZ * B, 4 * B), bf16),
            pltpu.VMEM((NZ * 2 * B, 2 * B), bf16),
            pltpu.VMEM((2, ROWS, B, 2 * B), f32),
            pltpu.VMEM((ROWS, B, 2 * B), f32),
            pltpu.VMEM((2, ROWS, B, B), bf16),
            pltpu.VMEM((ROWS, B, B), bf16),
            pltpu.VMEM((TILES, 8, B), i32),
            pltpu.VMEM((NZ, 8, B), i32),
            pltpu.VMEM((2, 8, B), i32),
            pltpu.SMEM((TILES, 8, B), i32),
            pltpu.SMEM((NZ, 8, B), i32),
            pltpu.SMEM((2, 8, B), i32),
            dma((3,)),
            dma((TILES + NZ,)), dma((TILES + NZ,)),
            dma((2, 4, 15)), dma((2, 4, 15)),
            dma((2, NZ - 1)), dma((2, NZ - 1)),
            dma((ROWS,)), dma((ROWS,)),
            dma((4, NZ - 1)), dma((4, NZ - 1)),
            dma((2,)), dma((2,)),
            dma((3,)),
        ],
        compiler_params=pltpu.CompilerParams(
            collective_id=1, has_side_effects=True, vmem_limit_bytes=56 * 1024 * 1024
        ),
    )(
        meta,
        f1_vals.reshape(ROWS, B, B),
        p0_vals.reshape(16, B, B),
        s_vals.reshape(16, B, B),
    )
    return p1, q.reshape(ROWS, 1, B, B)


def body(*args):
    p1, q, flag = fast(*args)
    return lax.cond(
        flag[0, 0] > 0,
        lambda p1, q, *args: dense(*args),
        lambda p1, q, *args: (p1, q),
        p1, q.reshape(ROWS, 1, B, B), *args,
    )


def solution(mesh):
    return jax.shard_map(
        body,
        mesh=mesh,
        in_specs=(
            P("row", ("col", "layer"), None, None),
            P("row", ("col", "layer")),
            P(("row", "layer"), "col", None, None),
            P(("row", "layer"), "col"),
            P(("row", "layer"), "col", None, None),
            P(("row", "layer"), "col"),
            P("row", ("col", "layer")),
            P("row", ("col", "layer")),
        ),
        out_specs=(P("row", ("col", "layer"), None, None), P("row", ("col", "layer"), None, None)),
        check_vma=False,
    )
```
